32 devices in a mesh: groups: 2 (over x), seq: 8 (over z, y), chan: 2 (over core).
Axes of the slice: x: 2, y: 2, z: 4, core: 2. Of those that a mesh axis runs over, the one named last changes fastest.
Arguments:
- query_feat: bfloat16 [4096, 2048], P('chan', ('groups', 'seq')), parts along dimension 1, may hold values from -6 to 6
- key_feat: bfloat16 [4096, 2048], P('chan', ('groups', 'seq')), parts along dimension 1, may hold values from -6 to 6
- value_feat: bfloat16 [4096, 2048], P('chan', ('groups', 'seq')), parts along dimension 1, may hold values from -6 to 6
- filter_seed: int32 [16], replicated, may hold values from 1 to 511
- filter_in: float32 [32, 64], replicated, may hold values from -1 to 1
- filter_bias: float32 [64], replicated, may hold values from -3.140625 to 3.140625
- filter_out: float32 [64, 256], P(None, 'chan'), may hold values from -0.75 to 0.75
- decay_rate: float32 [256], P('chan'), may hold values from 0.000390625 to 0.0078125
- reach_blocks: int32 [256], P('chan'), may hold values from 1 to 2, as said below
- skip_gain: float32 [4096], P('chan'), may hold values from -4 to 4
- out_weight: bfloat16 [4096, 2048], P('chan'), may hold values from -0.09375 to 0.09375
Outputs:
- projected: bfloat16 [2048, 2048], P(('groups', 'seq'), 'chan'), parts along dimension 0
The draws below stay inside these ranges and needn't reach their ends.
There are 2 independent parts, one for each index of `groups`. The reference program is written for one: setup_inputs(seed, part) draws one part's arguments, and reference() takes and returns one part's arrays. A program takes and returns all parts, laid end to end along the dimension named above; an argument that names none is the same for every part. Nothing has to cross between parts.
Inputs may be any that keep to these rules, and one draw needn't show every extreme that they name: `reach_blocks`: some filter group reaches 2 blocks and some filter group only one.
All inputs are finite; a program needn't handle non-finite values.
Results may differ from the reference program's by a relative error of at most 0.0059.
Values may be sent and summed in bfloat16 or wider, within the bound.
No kernel may reach another device: no remote copies, remote signals or barrier semaphores. Data moves between devices by JAX's collectives and lax.ppermute only.
A program may use at most 128 MiB of HBM per device.

```python
import math
import jax
import jax.numpy as jnp
from jax import lax

MODEL_DIM = 4096
FILTER_GROUPS = 256
OUT_COLS = 2048
POS_FREQS = 16
FILTER_HID = 64
BLOCK_TOK = 128
REACH_MAX = 2
SEQ_LEN = 1024


def draw_reach_blocks(key, part):
    values = jax.random.randint(jax.random.fold_in(key, 11), (FILTER_GROUPS,), 1, REACH_MAX + 1)
    top_place = jax.random.randint(jax.random.fold_in(key, 12), (), 0, FILTER_GROUPS)
    low_place = (top_place + jax.random.randint(jax.random.fold_in(key, 13), (), 1, FILTER_GROUPS)) % FILTER_GROUPS
    index = lax.iota(jnp.int32, FILTER_GROUPS)
    values = jnp.where(index == top_place, REACH_MAX, values)
    values = jnp.where(index == low_place, 1, values)
    return values.astype(jnp.int32)


def with_ends(entries, rng, smallest, largest):
    index_at = [jax.random.randint(jax.random.fold_in(rng, axis), (), 0, length) for axis, length in enumerate(entries.shape)]
    main_axis = entries.shape.index(max(entries.shape))
    neighbour = index_at[:main_axis] + [(index_at[main_axis] + 1) % entries.shape[main_axis]] + index_at[main_axis + 1:]
    return entries.at[tuple(index_at)].set(smallest).at[tuple(neighbour)].set(largest)


def shard_levels(own_key, dims, split, low, high):
    def one(position, parts):
        draws = jax.random.uniform(jax.random.fold_in(jax.random.fold_in(own_key, 6), position), (parts,), jnp.float32, low / len(split), high / len(split))
        return jnp.repeat(jnp.exp(draws), dims[position] // parts).reshape((-1,) + (1,) * (len(dims) - position - 1))

    gain = one(*split[0])
    for cut in split[1:]:
        gain = gain * one(*cut)
    return gain


def scatter_about(own_key, dims, width, most, cuts=(), dtype=jnp.bfloat16):
    array = jax.random.normal(own_key, dims, jnp.float32) * width
    if len(cuts) > 0:
        array = shard_levels(own_key, dims, cuts, -0.22, 0.18) * array
    return jnp.clip(array, min=-most, max=most).astype(dtype)


def setup_inputs(seed: int = 0, part: int = 0) -> dict:
    arg_keys = jax.random.split(jax.random.key(seed), 12)
    part_keys = jax.random.split(jax.random.fold_in(arg_keys[11], part), 12)
    return {
        "query_feat": scatter_about(part_keys[0], (MODEL_DIM, SEQ_LEN), 1.0, 6.0, ((0, 2), (1, 8))),
        "key_feat": scatter_about(part_keys[1], (MODEL_DIM, SEQ_LEN), 1.0, 6.0, ((0, 2), (1, 8))),
        "value_feat": scatter_about(part_keys[2], (MODEL_DIM, SEQ_LEN), 1.0, 6.0, ((0, 2), (1, 8))),
        "filter_seed": with_ends(jax.random.randint(arg_keys[3], (POS_FREQS,), 1, SEQ_LEN // 2), jax.random.fold_in(arg_keys[3], 1), 1, (SEQ_LEN // 2) - 1).astype(jnp.int32),
        "filter_in": scatter_about(arg_keys[4], (2 * POS_FREQS, FILTER_HID), (2 * POS_FREQS) ** -0.5, 1.0, (), jnp.float32),
        "filter_bias": jnp.clip(jax.random.uniform(arg_keys[5], (FILTER_HID,), jnp.float32, -3.140625, 3.140625), -3.140625, 3.140625),
        "filter_out": scatter_about(arg_keys[6], (FILTER_HID, FILTER_GROUPS), FILTER_HID ** -0.5, 0.75, ((1, 2),), jnp.float32),
        "decay_rate": jnp.clip(jnp.exp(math.log(0.0078125) - 2.9957323 * jax.random.uniform(arg_keys[7], (FILTER_GROUPS,), jnp.float32) ** shard_levels(arg_keys[7], (FILTER_GROUPS,), ((0, 2),), -0.2, 0.2)), 0.000390625, 0.0078125),
        "reach_blocks": draw_reach_blocks(jax.random.fold_in(arg_keys[11], 71), part),
        "skip_gain": scatter_about(arg_keys[9], (MODEL_DIM,), 1.0, 4.0, ((0, 2),), jnp.float32),
        "out_weight": scatter_about(arg_keys[10], (MODEL_DIM, OUT_COLS), MODEL_DIM ** -0.5, 0.09375, ((0, 2),)),
    }


def reference(query_feat, key_feat, value_feat, filter_seed, filter_in, filter_bias, filter_out, decay_rate, reach_blocks, skip_gain, out_weight):
    product = (key_feat.astype(jnp.float32) * value_feat.astype(jnp.float32)).astype(jnp.bfloat16)
    lag_index = lax.iota(jnp.int32, REACH_MAX * BLOCK_TOK)
    phases = lag_index[:, None] * filter_seed[None, :] % SEQ_LEN
    angles = phases.astype(jnp.float32) * (2.0 * math.pi / SEQ_LEN)
    features = jnp.concatenate([jnp.cos(angles), jnp.sin(angles)], axis=1)
    hidden = jnp.sin(jnp.dot(features, filter_in, precision=lax.Precision.HIGHEST, preferred_element_type=jnp.float32) + filter_bias)
    shaped = jnp.dot(hidden, filter_out, precision=lax.Precision.HIGHEST, preferred_element_type=jnp.float32)
    envelope = jnp.exp(-decay_rate[None, :] * lag_index.astype(jnp.float32)[:, None]) * (1.0 / math.sqrt(REACH_MAX * BLOCK_TOK))
    inside = lag_index[:, None] < reach_blocks[None, :] * BLOCK_TOK
    taps = jnp.where(inside, shaped * envelope, 0.0).astype(jnp.bfloat16)
    per_group = MODEL_DIM // FILTER_GROUPS
    fft_len = 2 * SEQ_LEN

    def convolve(inputs_pair):
        channel_rows, tap_row = inputs_pair
        spectrum = jnp.fft.rfft(channel_rows.astype(jnp.float32), n=fft_len, axis=1) * jnp.fft.rfft(tap_row.astype(jnp.float32), n=fft_len)[None, :]
        return jnp.fft.irfft(spectrum, n=fft_len, axis=1)[:, :SEQ_LEN]
    convolved = lax.map(convolve, (product.reshape(FILTER_GROUPS, per_group, SEQ_LEN), taps.T)).reshape(MODEL_DIM, SEQ_LEN)
    mixed = convolved + skip_gain[:, None] * product.astype(jnp.float32)
    gated = (query_feat.astype(jnp.float32) * mixed).astype(jnp.bfloat16)
    projected = lax.dot_general(gated, out_weight, (((0,), (0,)), ((), ())), preferred_element_type=jnp.float32)
    return projected.astype(jnp.bfloat16)
```

```python
import math

import jax
import jax.numpy as jnp
import numpy as np
from jax import lax
from jax.experimental import pallas as pl
from jax.experimental.pallas import tpu as pltpu
from jax.sharding import PartitionSpec as P

VMEM_BYTES = 32 * 1024 * 1024


def split_bf16(array):
    high = array.astype(jnp.bfloat16)
    low = (array - high.astype(np.float64)).astype(jnp.bfloat16)
    return high, low


def transform_tables(window, first_out, block):
    half = 128 * math.ceil(window / 256)
    omega = (np.arange(half) + 0.5) * (math.pi / half)
    angle = np.arange(window)[:, None] * omega[None, :]
    forward = np.concatenate([np.cos(angle), np.sin(angle)], axis=1)
    back = omega[:, None] * (first_out + np.arange(block))[None, :]
    inverse = np.concatenate([np.cos(back), np.sin(back)], axis=0) / half
    return split_bf16(forward), split_bf16(inverse)


def spectrum_kernel(seq_len, block, scale, seed, f_in, bias, f_out, decay, reach, fwd_hi, fwd_lo, out):
    lags = fwd_hi.shape[0]
    lag = lax.broadcasted_iota(jnp.int32, (lags, 1), 0)
    if seq_len & (seq_len - 1) == 0:
        phases = (lag * seed[...]) & (seq_len - 1)
    else:
        phases = lax.rem(lag * seed[...], seq_len)
    angles = phases.astype(jnp.float32) * (2.0 * math.pi / seq_len)
    features = jnp.concatenate([jnp.cos(angles), jnp.sin(angles)], axis=1)
    exact = dict(precision=lax.Precision.HIGHEST, preferred_element_type=jnp.float32)
    hidden = jnp.sin(jnp.dot(features, f_in[...], **exact) + bias[...])
    shaped = jnp.dot(hidden, f_out[...], **exact)
    envelope = jnp.exp(-decay[...] * lag.astype(jnp.float32)) * scale
    taps = jnp.where(lag < reach[...] * block, shaped * envelope, 0.0).astype(jnp.bfloat16)
    dims = (((0,), (0,)), ((), ()))
    out[...] = lax.dot_general(taps, fwd_hi[...], dims, preferred_element_type=jnp.float32) + lax.dot_general(
        taps, fwd_lo[...], dims, preferred_element_type=jnp.float32
    )


def conv_kernel(reach_max, per_group, core, *refs):
    xs = refs[: reach_max + 1]
    query, direct, spectrum, fwd_hi, fwd_lo, inverse, weight, part, gated_t, total, mult = refs[reach_max + 1 :]
    step = pl.program_id(0)
    half = fwd_hi.shape[1] // 2
    block = query.shape[1]
    window = jnp.concatenate([x[...] for x in xs], axis=1)
    freq = jnp.dot(window, fwd_hi[...], preferred_element_type=jnp.float32) + jnp.dot(
        window, fwd_lo[...], preferred_element_type=jnp.float32
    )
    for g in range(spectrum.shape[0]):
        rows = slice(g * per_group, (g + 1) * per_group)
        xc, xs_ = freq[rows, :half], freq[rows, half:]
        hc, hs = spectrum[g : g + 1, :half], spectrum[g : g + 1, half:]
        mult[rows, :half] = (xc * hc - xs_ * hs).astype(jnp.bfloat16)
        mult[rows, half:] = (xc * hs + xs_ * hc).astype(jnp.bfloat16)
    both = jnp.dot(mult[...], inverse[...], preferred_element_type=jnp.float32)
    mixed = both[:, :block] + both[:, block:] + direct[...]
    gated = (query[...].astype(jnp.float32) * mixed).astype(jnp.bfloat16).T
    gated_t[...] = gated

    @pl.when(step == 0)
    def _():
        total[...] = jnp.zeros_like(total)

    total[...] += jnp.dot(gated, weight[...], preferred_element_type=jnp.float32)

    @pl.when(step == pl.num_programs(0) - 1)
    def _():
        part[...] = total[...].astype(part.dtype)


def project_kernel(core, gated_t, weight, out):
    @pl.when(pl.program_id(0) == 0)
    def _():
        out[...] = jnp.zeros_like(out)

    out[...] += jnp.dot(gated_t[...], weight[...], preferred_element_type=jnp.float32)


def body(
    query_feat,
    key_feat,
    value_feat,
    filter_seed,
    filter_in,
    filter_bias,
    filter_out,
    decay_rate,
    reach_blocks,
    skip_gain,
    out_weight,
):
    channels, block = query_feat.shape
    seq_count = lax.axis_size("seq")
    reach_max = seq_count // 4
    filters = decay_rate.shape[0]
    per_group = channels // filters
    lags = reach_max * block
    window = lags + block
    (fwd_hi, fwd_lo), (inv_hi, inv_lo) = transform_tables(window, lags, block)
    inverse = np.concatenate([inv_hi, inv_lo], axis=1)
    length = fwd_hi.shape[1]
    cols = out_weight.shape[1] // 2
    params = pltpu.CompilerParams(vmem_limit_bytes=VMEM_BYTES)

    wide = key_feat.astype(jnp.float32) * value_feat.astype(jnp.float32)
    product = wide.astype(jnp.bfloat16)
    halos = [
        lax.ppermute(product, "seq", [(i, i + back) for i in range(seq_count - back)])
        for back in range(reach_max, 0, -1)
    ]
    direct = skip_gain[:, None] * product.astype(jnp.float32)

    spectrum = pl.pallas_call(
        lambda *refs: spectrum_kernel(block * seq_count, block, 1.0 / math.sqrt(lags), *refs),
        out_shape=jax.ShapeDtypeStruct((filters, length), jnp.float32),
        compiler_params=params,
    )(
        filter_seed[None],
        filter_in,
        filter_bias[None],
        filter_out,
        decay_rate[None],
        reach_blocks[None],
        jnp.asarray(fwd_hi[:lags]),
        jnp.asarray(fwd_lo[:lags]),
    )

    tile = math.gcd(256, channels)
    tiles = channels // tile
    core = lax.axis_index("chan").astype(jnp.int32).reshape(1)
    by_rows = lambda i, c: (i, 0)
    whole = lambda i, c: (0, 0)
    part, gated_t = pl.pallas_call(
        lambda core, *refs: conv_kernel(reach_max, per_group, core, *refs),
        grid_spec=pltpu.PrefetchScalarGridSpec(
            num_scalar_prefetch=1,
            grid=(tiles,),
            in_specs=[pl.BlockSpec((tile, block), by_rows)] * (reach_max + 3)
            + [
                pl.BlockSpec((tile // per_group, length), by_rows),
                pl.BlockSpec((window, length), whole),
                pl.BlockSpec((window, length), whole),
                pl.BlockSpec((length, 2 * block), whole),
                pl.BlockSpec((tile, cols), lambda i, c: (i, 1 - c[0])),
            ],
            out_specs=[
                pl.BlockSpec((block, cols), whole),
                pl.BlockSpec((block, tile), lambda i, c: (0, i)),
            ],
            scratch_shapes=[pltpu.VMEM((block, cols), jnp.float32), pltpu.VMEM((tile, length), jnp.bfloat16)],
        ),
        out_shape=[
            jax.ShapeDtypeStruct((block, cols), jnp.bfloat16),
            jax.ShapeDtypeStruct((block, channels), jnp.bfloat16),
        ],
        compiler_params=params,
    )(
        core,
        *halos,
        product,
        query_feat,
        direct,
        spectrum,
        jnp.asarray(fwd_hi),
        jnp.asarray(fwd_lo),
        jnp.asarray(inverse),
        out_weight,
    )
    received = lax.ppermute(part, "chan", [(0, 1), (1, 0)])
    own = pl.pallas_call(
        project_kernel,
        grid_spec=pltpu.PrefetchScalarGridSpec(
            num_scalar_prefetch=1,
            grid=(tiles,),
            in_specs=[
                pl.BlockSpec((block, tile), lambda i, c: (0, i)),
                pl.BlockSpec((tile, cols), lambda i, c: (i, c[0])),
            ],
            out_specs=pl.BlockSpec((block, cols), whole),
        ),
        out_shape=jax.ShapeDtypeStruct((block, cols), jnp.float32),
        compiler_params=params,
    )(core, gated_t, out_weight)
    return (own + received.astype(jnp.float32)).astype(jnp.bfloat16)


def solution(mesh):
    return jax.shard_map(
        body,
        mesh=mesh,
        in_specs=(
            P("chan", ("groups", "seq")),
            P("chan", ("groups", "seq")),
            P("chan", ("groups", "seq")),
            P(),
            P(),
            P(),
            P(None, "chan"),
            P("chan"),
            P("chan"),
            P("chan"),
            P("chan", None),
        ),
        out_specs=P(("groups", "seq"), "chan"),
        check_vma=False,
    )
```

```python
import math

import jax
import jax.numpy as jnp
import numpy as np
from jax import lax
from jax.experimental import pallas as pl
from jax.experimental.pallas import tpu as pltpu
from jax.sharding import PartitionSpec as P

SETUP_COST = 30_000_000
TAIL_COST = 1
VMEM_BYTES = 24 * 1024 * 1024
PART_A = 768


def split_bf16(array):
    high = array.astype(jnp.bfloat16)
    low = (array - high.astype(np.float64)).astype(jnp.bfloat16)
    return high, low


def transform_tables(window, first_out, block):
    half = 128 * math.ceil(window / 256)
    omega = (np.arange(half) + 0.5) * (math.pi / half)
    angle = np.arange(window)[:, None] * omega[None, :]
    forward = np.concatenate([np.cos(angle), np.sin(angle)], axis=1)
    back = omega[:, None] * (first_out + np.arange(block))[None, :]
    inverse = np.concatenate([np.cos(back), np.sin(back)], axis=0) / half
    return split_bf16(forward), split_bf16(inverse)


def setup_kernel(seq_len, block, scale, *refs):
    small, spectrum, local, sems = refs[:6], refs[10], refs[15:21], refs[21]
    table = refs[11]
    pairs = list(zip(small, local)) + list(zip(refs[6:10], refs[11:15]))
    copies = [pltpu.make_async_copy(source, target, sems.at[k]) for k, (source, target) in enumerate(pairs)]
    for copy in copies:
        copy.start()
    for copy in copies[:7]:
        copy.wait()
    seed, f_in, bias, f_out, decay, reach = local
    window = table.shape[0] // 2 - block
    lags = window - block
    lag = lax.broadcasted_iota(jnp.int32, (lags, 1), 0)
    if seq_len & (seq_len - 1) == 0:
        phases = (lag * seed[...]) & (seq_len - 1)
    else:
        phases = lax.rem(lag * seed[...], seq_len)
    angles = phases.astype(jnp.float32) * (2.0 * math.pi / seq_len)
    features = jnp.concatenate([jnp.cos(angles), jnp.sin(angles)], axis=1)
    exact = dict(precision=lax.Precision.HIGHEST, preferred_element_type=jnp.float32)
    hidden = jnp.sin(jnp.dot(features, f_in[...], **exact) + bias[...])
    shaped = jnp.dot(hidden, f_out[...], **exact)
    envelope = jnp.exp(-decay[...] * lag.astype(jnp.float32)) * scale
    taps = jnp.where(lag < reach[...] * block, shaped * envelope, 0.0).astype(jnp.bfloat16).T
    spectrum[...] = jnp.dot(taps, table[:lags], preferred_element_type=jnp.float32) + jnp.dot(
        taps, table[window : window + lags], preferred_element_type=jnp.float32
    )
    for copy in copies[7:]:
        copy.wait()


def convolve(first, per_group, xs, query, skip, spectrum, table, gated_t):
    channels, block = xs[0].shape
    half = table.shape[1] // 2
    depth = len(xs) * block
    tile = math.gcd(256, channels)
    for start in range(0, channels, tile):
        rows = slice(start, start + tile)
        window = jnp.concatenate([x[rows] for x in xs], axis=1)
        freq = jnp.dot(
            jnp.concatenate([window, window], axis=1), table[: 2 * depth], preferred_element_type=jnp.float32
        )
        mult = []
        for g in range(tile // per_group):
            part = freq[g * per_group : (g + 1) * per_group]
            group = (first + start) // per_group + g
            hc, hs = spectrum[group : group + 1, :half], spectrum[group : group + 1, half:]
            xc, xs_ = part[:, :half], part[:, half:]
            mult.append(jnp.concatenate([xc * hc - xs_ * hs, xc * hs + xs_ * hc], axis=1).astype(jnp.bfloat16))
        both = lax.dot_general(
            jnp.concatenate(mult, axis=0),
            table[2 * depth :],
            (((1,), (1,)), ((), ())),
            preferred_element_type=jnp.float32,
        )
        for low in range(0, tile, 128):
            row = (first + start + low) // 128
            gain = jnp.broadcast_to(skip[row : row + 1], (128, 128)).T
            if block != 128:
                gain = jnp.broadcast_to(gain[:, :1], (128, block))
            near = both[low : low + 128]
            here = slice(start + low, start + low + 128)
            mixed = near[:, :block] + near[:, block:] + gain * xs[-1][here].astype(jnp.float32)
            total = slice(first + start + low, first + start + low + 128)
            gated = (query[total].astype(jnp.float32) * mixed).astype(jnp.bfloat16)
            gated_t[:, here] = gated.T


def column_halves(weight):
    cols = weight.shape[1] // 2
    core = lax.axis_index("chan")
    return [pl.ds(pl.multiple_of(part * cols, 128), cols) for part in (core, 1 - core)]


def first_kernel(reach_max, per_group, *refs):
    xs = refs[: reach_max + 1]
    query, skip, spectrum, table, weight, part, own, gated_t = refs[reach_max + 1 :]
    convolve(0, per_group, xs, query, skip, spectrum, table, gated_t)
    here, there = column_halves(weight)
    depth = gated_t.shape[1]
    part[...] = jnp.dot(gated_t[...], weight[:depth, there], preferred_element_type=jnp.float32)
    own[...] = jnp.dot(gated_t[...], weight[:depth, here], preferred_element_type=jnp.float32)


def second_kernel(reach_max, per_group, first, *refs):
    xs = refs[: reach_max + 1]
    query, skip, spectrum, table, weight, before, part, gated_t = refs[reach_max + 1 :]
    convolve(first, per_group, xs, query, skip, spectrum, table, gated_t)
    depth = gated_t.shape[1]
    there = column_halves(weight)[1]
    total = before[...] + jnp.dot(
        gated_t[...], weight[first : first + depth, there], preferred_element_type=jnp.float32
    )
    part[...] = total.astype(part.dtype)


def own_kernel(first, gated_t, weight, before, out):
    here = column_halves(weight)[0]
    depth = gated_t.shape[1]
    out[...] = before[...] + jnp.dot(
        gated_t[...], weight[first : first + depth, here], preferred_element_type=jnp.float32
    )


def cost(bytes_accessed):
    return pl.CostEstimate(flops=1, bytes_accessed=bytes_accessed, transcendentals=0)


def shift(array, back):
    count = lax.axis_size("seq")
    return lax.ppermute(array, "seq", [(i, i + back) for i in range(count - back)])


def body(
    query_feat,
    key_feat,
    value_feat,
    filter_seed,
    filter_in,
    filter_bias,
    filter_out,
    decay_rate,
    reach_blocks,
    skip_gain,
    out_weight,
):
    channels, block = query_feat.shape
    seq_count = lax.axis_size("seq")
    reach_max = seq_count // 4
    filters = decay_rate.shape[0]
    per_group = channels // filters
    lags = reach_max * block
    window = lags + block
    (fwd_hi, fwd_lo), (inv_hi, inv_lo) = transform_tables(window, lags, block)
    table = np.concatenate([fwd_hi, fwd_lo, inv_hi.T, inv_lo.T], axis=0)
    length = table.shape[1]
    rows, out_cols = out_weight.shape
    cols = out_cols // 2
    params = pltpu.CompilerParams(vmem_limit_bytes=VMEM_BYTES)
    vmem = pl.BlockSpec(memory_space=pltpu.VMEM)
    f32, bf16 = jnp.float32, jnp.bfloat16
    shape = jax.ShapeDtypeStruct

    first = PART_A
    bounds = (slice(0, first), slice(first, channels))
    own_a, own_b = [
        (key_feat[cut].astype(f32) * value_feat[cut].astype(f32)).astype(bf16) for cut in bounds
    ]
    if reach_max == 2:
        far_a = shift(own_a, 2)
        odd = lax.axis_index("seq") % 2 == 1
        near_a = lax.ppermute(jnp.where(odd, far_a, own_a), "seq", [(i, i ^ 1) for i in range(seq_count)])
        halo_a = [far_a, near_a]
        halo_b = [shift(own_b, 2), shift(own_b, 1)]
    else:
        halo_a, halo_b = [[shift(own, back) for back in range(reach_max, 0, -1)] for own in (own_a, own_b)]

    small = (
        filter_seed[None],
        filter_in,
        filter_bias[None],
        filter_out,
        decay_rate[None],
        reach_blocks[None],
    )
    large = (
        jnp.asarray(table),
        out_weight,
        query_feat,
        skip_gain.reshape(-1, 128),
    )
    spectrum, table, weight, query, skip = pl.pallas_call(
        lambda *refs: setup_kernel(block * seq_count, block, 1.0 / math.sqrt(lags), *refs),
        in_specs=[pl.BlockSpec(memory_space=pltpu.HBM)] * 10,
        out_specs=[vmem] * 5,
        out_shape=[pltpu.VMEM((filters, length), f32)] + [pltpu.VMEM(a.shape, a.dtype) for a in large],
        scratch_shapes=[pltpu.VMEM(a.shape, a.dtype) for a in small] + [pltpu.SemaphoreType.DMA((10,))],
        compiler_params=params,
        cost_estimate=cost(SETUP_COST),
    )(*[pltpu.with_memory_space_constraint(a, pltpu.HBM) for a in small + large])
    common = (query, skip, spectrum, table)
    part_a, total_a = pl.pallas_call(
        lambda *refs: first_kernel(reach_max, per_group, *refs),
        in_specs=[vmem] * (reach_max + 6),
        out_specs=[vmem] * 2,
        out_shape=[shape((block, cols), f32)] * 2,
        scratch_shapes=[pltpu.VMEM((block, first), bf16)],
        compiler_params=params,
        cost_estimate=cost(TAIL_COST),
    )(*halo_a, own_a, *common, weight)
    part, gated_b = pl.pallas_call(
        lambda *refs: second_kernel(reach_max, per_group, first, *refs),
        in_specs=[vmem] * (reach_max + 7),
        out_specs=[vmem] * 2,
        out_shape=[shape((block, cols), bf16), shape((block, channels - first), bf16)],
        compiler_params=params,
        cost_estimate=cost(TAIL_COST),
    )(*halo_b, own_b, *common, weight, part_a)
    received = lax.ppermute(part, "chan", [(0, 1), (1, 0)])
    own = pl.pallas_call(
        lambda *refs: own_kernel(first, *refs),
        in_specs=[vmem] * 3,
        out_specs=vmem,
        out_shape=shape((block, cols), f32),
        compiler_params=params,
        cost_estimate=cost(TAIL_COST),
    )(gated_b, weight, total_a)
    return (own + received.astype(f32)).astype(bf16)


def solution(mesh):
    return jax.shard_map(
        body,
        mesh=mesh,
        in_specs=(
            P("chan", ("groups", "seq")),
            P("chan", ("groups", "seq")),
            P("chan", ("groups", "seq")),
            P(),
            P(),
            P(),
            P(None, "chan"),
            P("chan"),
            P("chan"),
            P("chan"),
            P("chan", None),
        ),
        out_specs=P(("groups", "seq"), "chan"),
        check_vma=False,
    )
```

```python
import functools
import math

import jax
import jax.numpy as jnp
import numpy as np
from jax import lax
from jax.experimental import pallas as pl
from jax.experimental.pallas import tpu as pltpu
from jax.sharding import PartitionSpec as P

SETUP_COST = 30_000_000
TAIL_COST = 1
VMEM_BYTES = 24 * 1024 * 1024
PARTS = (0, 768, 2048)
RELAYED = (True, False)
WRAP_FAR = True
WRAP_DIRECT = False


def split_bf16(array):
    high = array.astype(jnp.bfloat16)
    low = (array - high.astype(np.float64)).astype(jnp.bfloat16)
    return high, low


def transform_tables(window, first_out, block):
    half = 128 * math.ceil(window / 256)
    omega = (np.arange(half) + 0.5) * (math.pi / half)
    angle = np.arange(window)[:, None] * omega[None, :]
    forward = np.concatenate([np.cos(angle), np.sin(angle)], axis=1)
    back = omega[:, None] * (first_out + np.arange(block))[None, :]
    inverse = np.concatenate([np.cos(back), np.sin(back)], axis=0) / half
    return split_bf16(forward), split_bf16(inverse)


def setup_kernel(seq_len, block, scale, *refs):
    small, spectrum, local, sems = refs[:6], refs[10], refs[15:21], refs[21]
    table = refs[11]
    pairs = list(zip(small, local)) + list(zip(refs[6:10], refs[11:15]))
    copies = [pltpu.make_async_copy(source, target, sems.at[k]) for k, (source, target) in enumerate(pairs)]
    for copy in copies:
        copy.start()
    for copy in copies[:7]:
        copy.wait()
    seed, f_in, bias, f_out, decay, reach = local
    window = table.shape[0] // 2 - block
    lags = window - block
    lag = lax.broadcasted_iota(jnp.int32, (lags, 1), 0)
    if seq_len & (seq_len - 1) == 0:
        phases = (lag * seed[...]) & (seq_len - 1)
    else:
        phases = lax.rem(lag * seed[...], seq_len)
    angles = phases.astype(jnp.float32) * (2.0 * math.pi / seq_len)
    features = jnp.concatenate([jnp.cos(angles), jnp.sin(angles)], axis=1)
    exact = dict(precision=lax.Precision.HIGHEST, preferred_element_type=jnp.float32)
    hidden = jnp.sin(jnp.dot(features, f_in[...], **exact) + bias[...])
    shaped = jnp.dot(hidden, f_out[...], **exact)
    envelope = jnp.exp(-decay[...] * lag.astype(jnp.float32)) * scale
    taps = jnp.where(lag < reach[...] * block, shaped * envelope, 0.0).astype(jnp.bfloat16).T
    spectrum[...] = jnp.dot(taps, table[:lags], preferred_element_type=jnp.float32) + jnp.dot(
        taps, table[window : window + lags], preferred_element_type=jnp.float32
    )
    for copy in copies[7:]:
        copy.wait()


def convolve(first, per_group, xs, query, skip, spectrum, table, gated_t):
    channels, block = xs[0].shape
    half = table.shape[1] // 2
    depth = len(xs) * block
    seq = lax.axis_index("seq")
    for start in range(0, channels, 256):
        tile = min(256, channels - start)
        rows = slice(start, start + tile)
        blocks = [
            jnp.where(seq >= len(xs) - 1 - k, x[rows], jnp.zeros((tile, block), x.dtype))
            for k, x in enumerate(xs[:-1])
        ] + [xs[-1][rows]]
        freq = jnp.dot(
            jnp.concatenate(blocks + blocks, axis=1), table[: 2 * depth], preferred_element_type=jnp.float32
        )
        mult = []
        for g in range(tile // per_group):
            part = freq[g * per_group : (g + 1) * per_group]
            group = (first + start) // per_group + g
            hc, hs = spectrum[group : group + 1, :half], spectrum[group : group + 1, half:]
            xc, xs_ = part[:, :half], part[:, half:]
            mult.append(jnp.concatenate([xc * hc - xs_ * hs, xc * hs + xs_ * hc], axis=1).astype(jnp.bfloat16))
        both = lax.dot_general(
            jnp.concatenate(mult, axis=0),
            table[2 * depth :],
            (((1,), (1,)), ((), ())),
            preferred_element_type=jnp.float32,
        )
        for low in range(0, tile, 128):
            row = (first + start + low) // 128
            gain = jnp.broadcast_to(skip[row : row + 1], (128, 128)).T
            if block != 128:
                gain = jnp.broadcast_to(gain[:, :1], (128, block))
            near = both[low : low + 128]
            here = slice(start + low, start + low + 128)
            mixed = near[:, :block] + near[:, block:] + gain * xs[-1][here].astype(jnp.float32)
            total = slice(first + start + low, first + start + low + 128)
            gated = (query[total].astype(jnp.float32) * mixed).astype(jnp.bfloat16)
            gated_t[:, here] = gated.T


def column_halves(weight):
    cols = weight.shape[1] // 2
    core = lax.axis_index("chan")
    return [pl.ds(pl.multiple_of(part * cols, 128), cols) for part in (core, 1 - core)]


def part_kernel(blocks, per_group, first, is_first, is_last, *refs):
    xs, refs = refs[:blocks], refs[blocks:]
    (query, skip, spectrum, table, weight), refs = refs[:5], refs[5:]
    before, refs = ((), refs) if is_first else (refs[:1] if is_last else refs[:2], refs[1 if is_last else 2 :])
    outs, gated_t = refs[:-1], refs[-1]
    convolve(first, per_group, xs, query, skip, spectrum, table, gated_t)
    here, there = column_halves(weight)
    rows = slice(first, first + gated_t.shape[1])
    for k, columns in enumerate((there,) if is_last else (there, here)):
        total = jnp.dot(gated_t[...], weight[rows, columns], preferred_element_type=jnp.float32)
        if before:
            total = before[k][...] + total
        outs[k][...] = total.astype(outs[k].dtype)


def own_kernel(first, gated_t, weight, before, out):
    here = column_halves(weight)[0]
    depth = gated_t.shape[1]
    out[...] = before[...] + jnp.dot(
        gated_t[...], weight[first : first + depth, here], preferred_element_type=jnp.float32
    )


def cost(bytes_accessed):
    return pl.CostEstimate(flops=1, bytes_accessed=bytes_accessed, transcendentals=0)


def shift(array, back, cyclic):
    count = lax.axis_size("seq")
    return lax.ppermute(array, "seq", [(i, (i + back) % count) for i in range(count if cyclic else count - back)])


def swap_pairs(array):
    return lax.ppermute(array, "seq", [(i, i ^ 1) for i in range(lax.axis_size("seq"))])


def body(
    query_feat,
    key_feat,
    value_feat,
    filter_seed,
    filter_in,
    filter_bias,
    filter_out,
    decay_rate,
    reach_blocks,
    skip_gain,
    out_weight,
):
    channels, block = query_feat.shape
    seq_count = lax.axis_size("seq")
    reach_max = seq_count // 4
    filters = decay_rate.shape[0]
    per_group = channels // filters
    lags = reach_max * block
    window = lags + block
    (fwd_hi, fwd_lo), (inv_hi, inv_lo) = transform_tables(window, lags, block)
    table = np.concatenate([fwd_hi, fwd_lo, inv_hi.T, inv_lo.T], axis=0)
    length = table.shape[1]
    out_cols = out_weight.shape[1]
    cols = out_cols // 2
    params = pltpu.CompilerParams(vmem_limit_bytes=VMEM_BYTES)
    vmem = pl.BlockSpec(memory_space=pltpu.VMEM)
    f32, bf16 = jnp.float32, jnp.bfloat16
    shape = jax.ShapeDtypeStruct

    bounds = list(zip(PARTS[:-1], PARTS[1:]))
    products = [
        (key_feat[low:high].astype(f32) * value_feat[low:high].astype(f32)).astype(bf16) for low, high in bounds
    ]
    odd = lax.axis_index("seq") % 2 == 1
    windows = []
    for own, relayed in zip(products, RELAYED):
        if reach_max == 2 and relayed:
            far = shift(own, 2, WRAP_FAR)
            near = swap_pairs(jnp.where(odd, far, own))
            windows.append([far, near, own])
        else:
            windows.append([shift(own, back, WRAP_DIRECT) for back in range(reach_max, 0, -1)] + [own])

    small = (
        filter_seed[None],
        filter_in,
        filter_bias[None],
        filter_out,
        decay_rate[None],
        reach_blocks[None],
    )
    large = (
        jnp.asarray(table),
        out_weight,
        query_feat,
        skip_gain.reshape(-1, 128),
    )
    spectrum, table, weight, query, skip = pl.pallas_call(
        lambda *refs: setup_kernel(block * seq_count, block, 1.0 / math.sqrt(lags), *refs),
        in_specs=[pl.BlockSpec(memory_space=pltpu.HBM)] * 10,
        out_specs=[vmem] * 5,
        out_shape=[pltpu.VMEM((filters, length), f32)] + [pltpu.VMEM(a.shape, a.dtype) for a in large],
        scratch_shapes=[pltpu.VMEM(a.shape, a.dtype) for a in small] + [pltpu.SemaphoreType.DMA((10,))],
        compiler_params=params,
        cost_estimate=cost(SETUP_COST),
    )(*[pltpu.with_memory_space_constraint(a, pltpu.HBM) for a in small + large])

    common = (query, skip, spectrum, table, weight)
    sums = ()
    for k, ((low, high), blocks) in enumerate(zip(bounds, windows)):
        is_first, is_last = k == 0, k == len(bounds) - 1
        operands = (*blocks, *common, *(sums[:1] if is_last else sums))
        gated_shape = (block, high - low)
        results = pl.pallas_call(
            functools.partial(part_kernel, len(blocks), per_group, low, is_first, is_last),
            in_specs=[vmem] * len(operands),
            out_specs=[vmem] * 2,
            out_shape=[shape((block, cols), bf16), shape(gated_shape, bf16)]
            if is_last
            else [shape((block, cols), f32)] * 2,
            scratch_shapes=[] if is_last else [pltpu.VMEM(gated_shape, bf16)],
            compiler_params=params,
            cost_estimate=cost(TAIL_COST),
        )(*operands)
        if is_last:
            part, gated = results
        else:
            sums = results
    received = lax.ppermute(part, "chan", [(0, 1), (1, 0)])
    own = pl.pallas_call(
        functools.partial(own_kernel, bounds[-1][0]),
        in_specs=[vmem] * 3,
        out_specs=vmem,
        out_shape=shape((block, cols), f32),
        compiler_params=params,
        cost_estimate=cost(TAIL_COST),
    )(gated, weight, sums[1])
    return (own + received.astype(f32)).astype(bf16)


def solution(mesh):
    return jax.shard_map(
        body,
        mesh=mesh,
        in_specs=(
            P("chan", ("groups", "seq")),
            P("chan", ("groups", "seq")),
            P("chan", ("groups", "seq")),
            P(),
            P(),
            P(),
            P(None, "chan"),
            P("chan"),
            P("chan"),
            P("chan"),
            P("chan", None),
        ),
        out_specs=P(("groups", "seq"), "chan"),
        check_vma=False,
    )
```

```python
import functools
import math

import jax
import jax.numpy as jnp
import numpy as np
from jax import lax
from jax.experimental import pallas as pl
from jax.experimental.pallas import tpu as pltpu
from jax.sharding import PartitionSpec as P

SETUP_COST = 30_000_000
TAIL_COST = 1
VMEM_BYTES = 24 * 1024 * 1024
RELAYED = 768
FAR_CUTS = ()
ORDER = (0, 1)
EARLY_RELAYED = (0, 2)
EARLY_DIRECT = (1, 2)


def split_bf16(array):
    high = array.astype(jnp.bfloat16)
    low = (array - high.astype(np.float64)).astype(jnp.bfloat16)
    return high, low


def transform_tables(window, first_out, block):
    half = 128 * math.ceil(window / 256)
    omega = (np.arange(half) + 0.5) * (math.pi / half)
    angle = np.arange(window)[:, None] * omega[None, :]
    forward = np.concatenate([np.cos(angle), np.sin(angle)], axis=1)
    back = omega[:, None] * (first_out + np.arange(block))[None, :]
    inverse = np.concatenate([np.cos(back), np.sin(back)], axis=0) / half
    return split_bf16(forward), split_bf16(inverse)


def setup_kernel(seq_len, block, scale, *refs):
    small, spectrum, local, sems = refs[:6], refs[10], refs[15:21], refs[21]
    table = refs[11]
    pairs = list(zip(small, local)) + list(zip(refs[6:10], refs[11:15]))
    copies = [pltpu.make_async_copy(source, target, sems.at[k]) for k, (source, target) in enumerate(pairs)]
    for copy in copies:
        copy.start()
    for copy in copies[:7]:
        copy.wait()
    seed, f_in, bias, f_out, decay, reach = local
    window = table.shape[0] // 2 - block
    lags = window - block
    lag = lax.broadcasted_iota(jnp.int32, (lags, 1), 0)
    if seq_len & (seq_len - 1) == 0:
        phases = (lag * seed[...]) & (seq_len - 1)
    else:
        phases = lax.rem(lag * seed[...], seq_len)
    angles = phases.astype(jnp.float32) * (2.0 * math.pi / seq_len)
    features = jnp.concatenate([jnp.cos(angles), jnp.sin(angles)], axis=1)
    exact = dict(precision=lax.Precision.HIGHEST, preferred_element_type=jnp.float32)
    hidden = jnp.sin(jnp.dot(features, f_in[...], **exact) + bias[...])
    shaped = jnp.dot(hidden, f_out[...], **exact)
    envelope = jnp.exp(-decay[...] * lag.astype(jnp.float32)) * scale
    taps = jnp.where(lag < reach[...] * block, shaped * envelope, 0.0).astype(jnp.bfloat16).T
    spectrum[...] = jnp.dot(taps, table[:lags], preferred_element_type=jnp.float32) + jnp.dot(
        taps, table[window : window + lags], preferred_element_type=jnp.float32
    )
    for copy in copies[7:]:
        copy.wait()


def transform(window, places, offsets, xs, table, start, tile):
    block = xs[0].shape[1]
    oldest = window // block - 1
    seq = lax.axis_index("seq")
    blocks, factors = [], []
    for place, offset, x in zip(places, offsets, xs):
        rows = x[offset + start : offset + start + tile]
        if place < oldest:
            rows = jnp.where(seq >= oldest - place, rows, jnp.zeros_like(rows))
        blocks.append(rows)
    for base in (0, window):
        factors += [table[base + place * block : base + (place + 1) * block] for place in places]
    return jnp.dot(
        jnp.concatenate(blocks + blocks, axis=1),
        jnp.concatenate(factors, axis=0),
        preferred_element_type=jnp.float32,
    )


def early_kernel(window, places, offsets, *refs):
    xs, (table, out) = refs[: len(places)], refs[len(places) :]
    channels = out.shape[0]
    for start in range(0, channels, 256):
        tile = min(256, channels - start)
        out[start : start + tile] = transform(window, places, offsets, xs, table, start, tile)


def convolve(first, window, places, offsets, per_group, xs, early, own, own_offset, query, skip, spectrum, table, gated_t):
    block, channels = gated_t.shape
    half = table.shape[1] // 2
    for start in range(0, channels, 256):
        tile = min(256, channels - start)
        freq = early[start : start + tile] + transform(window, places, offsets, xs, table, start, tile)
        mult = []
        for g in range(tile // per_group):
            part = freq[g * per_group : (g + 1) * per_group]
            group = (first + start) // per_group + g
            hc, hs = spectrum[group : group + 1, :half], spectrum[group : group + 1, half:]
            xc, xs_ = part[:, :half], part[:, half:]
            mult.append(jnp.concatenate([xc * hc - xs_ * hs, xc * hs + xs_ * hc], axis=1).astype(jnp.bfloat16))
        both = lax.dot_general(
            jnp.concatenate(mult, axis=0),
            table[2 * window :],
            (((1,), (1,)), ((), ())),
            preferred_element_type=jnp.float32,
        )
        for low in range(0, tile, 128):
            row = (first + start + low) // 128
            gain = jnp.broadcast_to(skip[row : row + 1], (128, 128)).T
            if block != 128:
                gain = jnp.broadcast_to(gain[:, :1], (128, block))
            near = both[low : low + 128]
            product = own[own_offset + start + low : own_offset + start + low + 128]
            here = slice(start + low, start + low + 128)
            mixed = near[:, :block] + near[:, block:] + gain * product.astype(jnp.float32)
            total = slice(first + start + low, first + start + low + 128)
            gated = (query[total].astype(jnp.float32) * mixed).astype(jnp.bfloat16)
            gated_t[:, here] = gated.T


def column_halves(weight):
    cols = weight.shape[1] // 2
    core = lax.axis_index("chan")
    return [pl.ds(pl.multiple_of(part * cols, 128), cols) for part in (core, 1 - core)]


def part_kernel(window, places, offsets, own_offset, per_group, first, is_first, is_last, *refs):
    xs, (early, own), refs = refs[: len(places)], refs[len(places) : len(places) + 2], refs[len(places) + 2 :]
    (query, skip, spectrum, table, weight), refs = refs[:5], refs[5:]
    before, refs = ((), refs) if is_first else (refs[:1] if is_last else refs[:2], refs[1 if is_last else 2 :])
    outs, gated_t = refs[:-1], refs[-1]
    convolve(
        first, window, places, offsets, per_group, xs, early, own, own_offset, query, skip, spectrum, table, gated_t
    )
    here, there = column_halves(weight)
    rows = slice(first, first + gated_t.shape[1])
    for k, columns in enumerate((there,) if is_last else (there, here)):
        total = jnp.dot(gated_t[...], weight[rows, columns], preferred_element_type=jnp.float32)
        if before:
            total = before[k][...] + total
        outs[k][...] = total.astype(outs[k].dtype)


def own_kernel(first, gated_t, weight, before, out):
    here = column_halves(weight)[0]
    depth = gated_t.shape[1]
    out[...] = before[...] + jnp.dot(
        gated_t[...], weight[first : first + depth, here], preferred_element_type=jnp.float32
    )


def cost(bytes_accessed):
    return pl.CostEstimate(flops=1, bytes_accessed=bytes_accessed, transcendentals=0)


def shift(array, back, cyclic):
    count = lax.axis_size("seq")
    return lax.ppermute(array, "seq", [(i, (i + back) % count) for i in range(count if cyclic else count - back)])


def swap_pairs(array):
    return lax.ppermute(array, "seq", [(i, i ^ 1) for i in range(lax.axis_size("seq"))])


def body(
    query_feat,
    key_feat,
    value_feat,
    filter_seed,
    filter_in,
    filter_bias,
    filter_out,
    decay_rate,
    reach_blocks,
    skip_gain,
    out_weight,
):
    channels, block = query_feat.shape
    seq_count = lax.axis_size("seq")
    reach_max = seq_count // 4
    filters = decay_rate.shape[0]
    per_group = channels // filters
    lags = reach_max * block
    window = lags + block
    (fwd_hi, fwd_lo), (inv_hi, inv_lo) = transform_tables(window, lags, block)
    table = np.concatenate([fwd_hi, fwd_lo, inv_hi.T, inv_lo.T], axis=0)
    length = table.shape[1]
    out_cols = out_weight.shape[1]
    cols = out_cols // 2
    params = pltpu.CompilerParams(vmem_limit_bytes=VMEM_BYTES)
    vmem = pl.BlockSpec(memory_space=pltpu.VMEM)
    f32, bf16 = jnp.float32, jnp.bfloat16
    shape = jax.ShapeDtypeStruct

    products = [
        (key_feat[low:high].astype(f32) * value_feat[low:high].astype(f32)).astype(bf16)
        for low, high in ((0, RELAYED), (RELAYED, channels))
    ]
    parts = []
    if reach_max == 2:
        own = products[0]
        far = shift(own, 2, True)
        near = swap_pairs(jnp.where(lax.axis_index("seq") % 2 == 1, far, own))
        parts.append((0, RELAYED, EARLY_RELAYED, [(far, 0), (near, 0), (own, 0)]))
        own = products[1]
        near = shift(own, 1, False)
        for low, high in zip((0,) + FAR_CUTS, FAR_CUTS + (channels - RELAYED,)):
            far = shift(own[low:high], 2, True)
            parts.append((RELAYED + low, RELAYED + high, EARLY_DIRECT, [(far, 0), (near, low), (own, low)]))
        parts = [parts[k] for k in ORDER]
    else:
        for own, low, high in zip(products, (0, RELAYED), (RELAYED, channels)):
            halo = [shift(own, back, False) for back in range(reach_max, 0, -1)]
            parts.append((low, high, [reach_max], [(array, 0) for array in (*halo, own)]))

    small = (
        filter_seed[None],
        filter_in,
        filter_bias[None],
        filter_out,
        decay_rate[None],
        reach_blocks[None],
    )
    large = (
        jnp.asarray(table),
        out_weight,
        query_feat,
        skip_gain.reshape(-1, 128),
    )
    spectrum, table, weight, query, skip = pl.pallas_call(
        lambda *refs: setup_kernel(block * seq_count, block, 1.0 / math.sqrt(lags), *refs),
        in_specs=[pl.BlockSpec(memory_space=pltpu.HBM)] * 10,
        out_specs=[vmem] * 5,
        out_shape=[pltpu.VMEM((filters, length), f32)] + [pltpu.VMEM(a.shape, a.dtype) for a in large],
        scratch_shapes=[pltpu.VMEM(a.shape, a.dtype) for a in small] + [pltpu.SemaphoreType.DMA((10,))],
        compiler_params=params,
        cost_estimate=cost(SETUP_COST),
    )(*[pltpu.with_memory_space_constraint(a, pltpu.HBM) for a in small + large])

    common = (query, skip, spectrum, table, weight)
    sums = ()
    for k, (low, high, before, blocks) in enumerate(parts):
        is_first, is_last = k == 0, k == len(parts) - 1
        now = [place for place in range(reach_max + 1) if place not in before]
        early = pl.pallas_call(
            functools.partial(early_kernel, window, before, [blocks[place][1] for place in before]),
            in_specs=[vmem] * (len(before) + 1),
            out_specs=vmem,
            out_shape=shape((high - low, length), f32),
            compiler_params=params,
            cost_estimate=cost(TAIL_COST),
        )(*[blocks[place][0] for place in before], table)
        operands = (
            *[blocks[place][0] for place in now],
            early,
            blocks[-1][0],
            *common,
            *(sums[:1] if is_last else sums),
        )
        offsets = [blocks[place][1] for place in now]
        gated_shape = (block, high - low)
        results = pl.pallas_call(
            functools.partial(part_kernel, window, now, offsets, blocks[-1][1], per_group, low, is_first, is_last),
            in_specs=[vmem] * len(operands),
            out_specs=[vmem] * 2,
            out_shape=[shape((block, cols), bf16), shape(gated_shape, bf16)]
            if is_last
            else [shape((block, cols), f32)] * 2,
            scratch_shapes=[] if is_last else [pltpu.VMEM(gated_shape, bf16)],
            compiler_params=params,
            cost_estimate=cost(TAIL_COST),
        )(*operands)
        if is_last:
            part, gated = results
        else:
            sums = results
    received = lax.ppermute(part, "chan", [(0, 1), (1, 0)])
    own = pl.pallas_call(
        functools.partial(own_kernel, parts[-1][0]),
        in_specs=[vmem] * 3,
        out_specs=vmem,
        out_shape=shape((block, cols), f32),
        compiler_params=params,
        cost_estimate=cost(TAIL_COST),
    )(gated, weight, sums[1])
    return (own + received.astype(f32)).astype(bf16)


def solution(mesh):
    return jax.shard_map(
        body,
        mesh=mesh,
        in_specs=(
            P("chan", ("groups", "seq")),
            P("chan", ("groups", "seq")),
            P("chan", ("groups", "seq")),
            P(),
            P(),
            P(),
            P(None, "chan"),
            P("chan"),
            P("chan"),
            P("chan"),
            P("chan", None),
        ),
        out_specs=P(("groups", "seq"), "chan"),
        check_vma=False,
    )
```

```python
import functools
import math

import jax
import jax.numpy as jnp
import numpy as np
from jax import lax
from jax.experimental import pallas as pl
from jax.experimental.pallas import tpu as pltpu
from jax.sharding import PartitionSpec as P

SETUP_COST = 30_000_000
TAIL_COST = 1
VMEM_BYTES = 24 * 1024 * 1024
RELAYED = 1024
WRAP_FAR = False
WRAP_SENT = True


def split_bf16(array):
    high = array.astype(jnp.bfloat16)
    low = (array - high.astype(np.float64)).astype(jnp.bfloat16)
    return high, low


def transform_tables(window, first_out, block):
    half = 128 * math.ceil(window / 256)
    omega = (np.arange(half) + 0.5) * (math.pi / half)
    angle = np.arange(window)[:, None] * omega[None, :]
    forward = np.concatenate([np.cos(angle), np.sin(angle)], axis=1)
    back = omega[:, None] * (first_out + np.arange(block))[None, :]
    inverse = np.concatenate([np.cos(back), np.sin(back)], axis=0) / half
    return split_bf16(forward), split_bf16(inverse)


def setup_kernel(seq_len, block, scale, *refs):
    small, weight, spectrum, weight_out, local, sems = refs[:6], refs[9], refs[10], refs[14], refs[15:21], refs[21]
    table = refs[11]
    pairs = list(zip(small, local)) + list(zip(refs[6:9], refs[11:14]))
    pairs.append((weight.at[: weight_out.shape[0]], weight_out))
    copies = [pltpu.make_async_copy(source, target, sems.at[k]) for k, (source, target) in enumerate(pairs)]
    for copy in copies:
        copy.start()
    for copy in copies[:7]:
        copy.wait()
    seed, f_in, bias, f_out, decay, reach = local
    window = table.shape[0] // 2 - block
    lags = window - block
    lag = lax.broadcasted_iota(jnp.int32, (lags, 1), 0)
    if seq_len & (seq_len - 1) == 0:
        phases = (lag * seed[...]) & (seq_len - 1)
    else:
        phases = lax.rem(lag * seed[...], seq_len)
    angles = phases.astype(jnp.float32).T * (2.0 * math.pi / seq_len)
    features = jnp.concatenate([jnp.cos(angles), jnp.sin(angles)], axis=0)
    dims = (((0,), (0,)), ((), ()))
    exact = dict(precision=lax.Precision.HIGHEST, preferred_element_type=jnp.float32)
    shift = jnp.broadcast_to(bias[...], (8, bias.shape[1])).T[:, :1]
    hidden = jnp.sin(lax.dot_general(f_in[...], features, dims, **exact) + shift)
    shaped = lax.dot_general(hidden, f_out[...], dims, **exact)
    envelope = jnp.exp(-decay[...] * lag.astype(jnp.float32)) * scale
    taps = jnp.where(lag < reach[...] * block, shaped * envelope, 0.0).astype(jnp.bfloat16).T
    spectrum[...] = jnp.dot(taps, table[:lags], preferred_element_type=jnp.float32) + jnp.dot(
        taps, table[window : window + lags], preferred_element_type=jnp.float32
    )
    for copy in copies[7:]:
        copy.wait()


def transform(window, places, offsets, xs, valid, table, start, tile):
    block = xs[0].shape[1]
    blocks, factors = [], []
    for offset, x, there in zip(offsets, xs, valid):
        rows = x[offset + start : offset + start + tile]
        blocks.append(rows if there is None else jnp.where(there, rows, jnp.zeros_like(rows)))
    for base in (0, window):
        factors += [table[base + place * block : base + (place + 1) * block] for place in places]
    return jnp.dot(
        jnp.concatenate(blocks + blocks, axis=1),
        jnp.concatenate(factors, axis=0),
        preferred_element_type=jnp.float32,
    )


def block_there(window, block, place):
    back = window // block - 1 - place
    return None if back == 0 else lax.axis_index("seq") >= back


def respond(freq, group, per_group, window, spectrum, table):
    half = table.shape[1] // 2
    mult = []
    for g in range(freq.shape[0] // per_group):
        part = freq[g * per_group : (g + 1) * per_group]
        hc, hs = spectrum[group + g : group + g + 1, :half], spectrum[group + g : group + g + 1, half:]
        xc, xs = part[:, :half], part[:, half:]
        mult.append(jnp.concatenate([xc * hc - xs * hs, xc * hs + xs * hc], axis=1).astype(jnp.bfloat16))
    both = lax.dot_general(
        jnp.concatenate(mult, axis=0),
        table[2 * window :],
        (((1,), (1,)), ((), ())),
        preferred_element_type=jnp.float32,
    )
    block = both.shape[1] // 2
    return both[:, :block] + both[:, block:]


def tiles_of(channels):
    return [(start, min(256, channels - start)) for start in range(0, channels, 256)]


def early_kernel(window, places, *refs):
    xs, (table, *fetch) = refs[: len(places)], refs[len(places) :]
    if len(fetch) > 1:
        weight, out, weight_out, sem = fetch
        copy = pltpu.make_async_copy(weight.at[weight.shape[0] - weight_out.shape[0] :], weight_out, sem)
        copy.start()
    else:
        (out,), copy = fetch, None
    valid = [block_there(window, xs[0].shape[1], place) for place in places]
    for start, tile in tiles_of(out.shape[0]):
        out[start : start + tile] = transform(window, places, [0] * len(xs), xs, valid, table, start, tile)
    if copy is not None:
        copy.wait()


def ahead_kernel(window, per_group, first, own, other, spectrum, table, out):
    even = lax.axis_index("seq") % 2 == 0
    for start, tile in tiles_of(out.shape[0]):
        freq = transform(window, (0, 1), (0, 0), (own, other), (None, even), table, start, tile)
        ahead = respond(freq, (first + start) // per_group, per_group, window, spectrum, table)
        out[start : start + tile] = ahead.astype(out.dtype)


def gains(skip, row, block):
    gain = jnp.broadcast_to(skip[row : row + 1], (128, 128)).T
    return gain if block == 128 else jnp.broadcast_to(gain[:, :1], (128, block))


def base_kernel(window, per_group, first, other, own, skip, spectrum, table, out):
    oldest = window // own.shape[1] - 1
    odd = lax.axis_index("seq") % 2 == 1
    for start, tile in tiles_of(out.shape[0]):
        freq = transform(window, (oldest - 1, oldest), (0, 0), (other, own), (odd, None), table, start, tile)
        mixed = respond(freq, (first + start) // per_group, per_group, window, spectrum, table)
        for low in range(0, tile, 128):
            here = slice(start + low, start + low + 128)
            gain = gains(skip, (first + start + low) // 128, own.shape[1])
            out[here] = mixed[low : low + 128] + gain * own[here].astype(jnp.float32)


def last_kernel(first, carried, base, query, weight, before, part, gated_t):
    there = column_halves(weight)[1]
    arrived = lax.axis_index("seq") >= 2
    for start, tile in tiles_of(base.shape[0]):
        rows = slice(start, start + tile)
        mixed = base[rows] + jnp.where(arrived, carried[rows].astype(jnp.float32), 0.0)
        gated = query[first + start : first + start + tile].astype(jnp.float32) * mixed
        gated_t[:, rows] = gated.astype(jnp.bfloat16).T
    total = jnp.dot(gated_t[...], weight[:, there], preferred_element_type=jnp.float32)
    part[...] = (before[...] + total).astype(part.dtype)


def column_halves(weight):
    cols = weight.shape[1] // 2
    core = lax.axis_index("chan")
    return [pl.ds(pl.multiple_of(part * cols, 128), cols) for part in (core, 1 - core)]


def hand_kernel(far, own, out):
    out[...] = jnp.where(lax.axis_index("seq") % 2 == 1, far[...], own[...])


def part_kernel(window, places, per_group, first, is_first, *refs):
    xs, refs = refs[: len(places)], refs[len(places) :]
    (early, own, query, skip, spectrum, table, weight), refs = refs[:7], refs[7:]
    part, gated_t = refs[-2:]
    block, channels = gated_t.shape
    valid = [block_there(window, block, place) for place in places]
    for start, tile in tiles_of(channels):
        freq = early[start : start + tile] + transform(window, places, [0] * len(xs), xs, valid, table, start, tile)
        mixed = respond(freq, (first + start) // per_group, per_group, window, spectrum, table)
        for low in range(0, tile, 128):
            here = slice(start + low, start + low + 128)
            total = slice(first + start + low, first + start + low + 128)
            gain = gains(skip, (first + start + low) // 128, block)
            sums = mixed[low : low + 128] + gain * own[here].astype(jnp.float32)
            gated_t[:, here] = (query[total].astype(jnp.float32) * sums).astype(jnp.bfloat16).T
    there = column_halves(weight)[1]
    total = jnp.dot(gated_t[...], weight[:, there], preferred_element_type=jnp.float32)
    if not is_first:
        total = refs[0][...] + total
    part[...] = total.astype(part.dtype)


def own_kernel(gated_a, gated_b, weight_a, weight_b, out):
    here = column_halves(weight_a)[0]
    out[...] = jnp.dot(gated_a[...], weight_a[:, here], preferred_element_type=jnp.float32) + jnp.dot(
        gated_b[...], weight_b[:, here], preferred_element_type=jnp.float32
    )


def cost(bytes_accessed):
    return pl.CostEstimate(flops=1, bytes_accessed=bytes_accessed, transcendentals=0)


def shift(array, back, cyclic):
    count = lax.axis_size("seq")
    return lax.ppermute(array, "seq", [(i, (i + back) % count) for i in range(count if cyclic else count - back)])


def swap_pairs(array):
    return lax.ppermute(array, "seq", [(i, i ^ 1) for i in range(lax.axis_size("seq"))])


def body(
    query_feat,
    key_feat,
    value_feat,
    filter_seed,
    filter_in,
    filter_bias,
    filter_out,
    decay_rate,
    reach_blocks,
    skip_gain,
    out_weight,
):
    channels, block = query_feat.shape
    seq_count = lax.axis_size("seq")
    reach_max = seq_count // 4
    filters = decay_rate.shape[0]
    per_group = channels // filters
    lags = reach_max * block
    window = lags + block
    (fwd_hi, fwd_lo), (inv_hi, inv_lo) = transform_tables(window, lags, block)
    table = np.concatenate([fwd_hi, fwd_lo, inv_hi.T, inv_lo.T], axis=0)
    length = table.shape[1]
    out_cols = out_weight.shape[1]
    cols = out_cols // 2
    params = pltpu.CompilerParams(vmem_limit_bytes=VMEM_BYTES)
    vmem = pl.BlockSpec(memory_space=pltpu.VMEM)
    f32, bf16 = jnp.float32, jnp.bfloat16
    shape = jax.ShapeDtypeStruct

    products = [
        (key_feat[low:high].astype(f32) * value_feat[low:high].astype(f32)).astype(bf16)
        for low, high in ((0, RELAYED), (RELAYED, channels))
    ]
    if reach_max == 2:
        other = swap_pairs(products[1])
        far = shift(products[0], 2, WRAP_FAR)

    small = (
        filter_seed[None],
        filter_in,
        filter_bias[None],
        filter_out,
        decay_rate[None],
        reach_blocks[None],
    )
    large = (
        jnp.asarray(table),
        query_feat,
        skip_gain.reshape(-1, 128),
    )
    weight_in = pltpu.with_memory_space_constraint(out_weight, pltpu.HBM)
    spectrum, table, query, skip, weight = pl.pallas_call(
        lambda *refs: setup_kernel(block * seq_count, block, 1.0 / math.sqrt(lags), *refs),
        in_specs=[pl.BlockSpec(memory_space=pltpu.HBM)] * 10,
        out_specs=[vmem] * 5,
        out_shape=[pltpu.VMEM((filters, length), f32)] + [pltpu.VMEM(a.shape, a.dtype) for a in large]
        + [pltpu.VMEM((RELAYED, out_cols), bf16)],
        scratch_shapes=[pltpu.VMEM(a.shape, a.dtype) for a in small] + [pltpu.SemaphoreType.DMA((10,))],
        compiler_params=params,
        cost_estimate=cost(SETUP_COST),
    )(*[pltpu.with_memory_space_constraint(a, pltpu.HBM) for a in small + large], weight_in)

    def kernel(call, ins, *outs, fetch=None):
        return pl.pallas_call(
            call,
            in_specs=[vmem] * len(ins) + [pl.BlockSpec(memory_space=pltpu.HBM)] * (fetch is not None),
            out_specs=[vmem] * len(outs),
            out_shape=outs,
            scratch_shapes=[pltpu.SemaphoreType.DMA] * (fetch is not None),
            compiler_params=params,
            cost_estimate=cost(TAIL_COST),
        )(*ins, *[weight_in] * (fetch is not None))

    def early(own, before, fetch=None):
        outs = [shape((own.shape[0], length), f32)]
        if fetch is not None:
            outs.append(pltpu.VMEM((fetch, out_cols), bf16))
        call = functools.partial(early_kernel, window, tuple(before))
        return kernel(call, (*before.values(), table), *outs, fetch=fetch)

    def part(own, first, late, transformed, weight, sums, dtype):
        ins = (*late.values(), transformed, own, query, skip, spectrum, table, weight, *sums)
        call = functools.partial(part_kernel, window, tuple(late), per_group, first, not sums)
        return kernel(call, ins, shape((block, cols), dtype), shape((block, own.shape[0]), bf16))

    own_a, own_b = products
    rest = channels - RELAYED
    if reach_max == 2:
        (sent,) = kernel(
            functools.partial(ahead_kernel, window, per_group, RELAYED),
            (own_b, other, spectrum, table),
            shape(own_b.shape, bf16),
        )
        carried = shift(sent, 2, WRAP_SENT)
        ready, _ = lax.optimization_barrier((own_a, sent))
        (handed,) = kernel(hand_kernel, (far, ready), shape(own_a.shape, bf16))
        near = swap_pairs(handed)
        transformed, weight_b = early(own_a, {0: far, 2: own_a}, rest)
        (base,) = kernel(
            functools.partial(base_kernel, window, per_group, RELAYED),
            (other, own_b, skip, spectrum, table),
            shape(own_b.shape, f32),
        )
        sums, gated_a = part(own_a, 0, {1: near}, transformed, weight, (), f32)
        sums, gated_b = kernel(
            functools.partial(last_kernel, RELAYED),
            (carried, base, query, weight_b, sums),
            shape((block, cols), bf16),
            shape((block, rest), bf16),
        )
    else:
        halos = [{reach_max - back: shift(own, back, False) for back in range(1, reach_max + 1)} for own in products]
        transformed, weight_b = early(own_a, {reach_max: own_a}, rest)
        sums, gated_a = part(own_a, 0, halos[0], transformed, weight, (), f32)
        (transformed,) = early(own_b, {reach_max: own_b})
        sums, gated_b = part(own_b, RELAYED, halos[1], transformed, weight_b, (sums,), bf16)
    received = lax.ppermute(sums, "chan", [(0, 1), (1, 0)])
    (own,) = kernel(own_kernel, (gated_a, gated_b, weight, weight_b), shape((block, cols), f32))
    return (own + received.astype(f32)).astype(bf16)


def solution(mesh):
    return jax.shard_map(
        body,
        mesh=mesh,
        in_specs=(
            P("chan", ("groups", "seq")),
            P("chan", ("groups", "seq")),
            P("chan", ("groups", "seq")),
            P(),
            P(),
            P(),
            P(None, "chan"),
            P("chan"),
            P("chan"),
            P("chan"),
            P("chan", None),
        ),
        out_specs=P(("groups", "seq"), "chan"),
        check_vma=False,
    )
```

```python
import functools
import math

import jax
import jax.numpy as jnp
import numpy as np
from jax import lax
from jax.experimental import pallas as pl
from jax.experimental.pallas import tpu as pltpu
from jax.sharding import PartitionSpec as P

SETUP_COST = 30_000_000
TAIL_COST = 1
VMEM_BYTES = 24 * 1024 * 1024
RELAYED = 1024
WRAP_FAR = True
WRAP_SENT = False


def split_bf16(array):
    high = array.astype(jnp.bfloat16)
    low = (array - high.astype(np.float64)).astype(jnp.bfloat16)
    return high, low


def transform_tables(window, first_out, block):
    half = 128 * math.ceil(window / 256)
    omega = (np.arange(half) + 0.5) * (math.pi / half)
    angle = np.arange(window)[:, None] * omega[None, :]
    forward = np.concatenate([np.cos(angle), np.sin(angle)], axis=1)
    back = omega[:, None] * (first_out + np.arange(block))[None, :]
    inverse = np.concatenate([np.cos(back), np.sin(back)], axis=0) / half
    return split_bf16(forward), split_bf16(inverse)


def setup_kernel(seq_len, block, scale, *refs):
    small, weight, spectrum, weight_out, local, sems = refs[:6], refs[9], refs[10], refs[14], refs[15:21], refs[21]
    table = refs[11]
    pairs = list(zip(small, local)) + list(zip(refs[6:9], refs[11:14]))
    pairs.append((weight, weight_out))
    copies = [pltpu.make_async_copy(source, target, sems.at[k]) for k, (source, target) in enumerate(pairs)]
    for copy in copies:
        copy.start()
    for copy in copies[:7]:
        copy.wait()
    seed, f_in, bias, f_out, decay, reach = local
    window = table.shape[0] // 2 - block
    lags = window - block
    lag = lax.broadcasted_iota(jnp.int32, (lags, 1), 0)
    if seq_len & (seq_len - 1) == 0:
        phases = (lag * seed[...]) & (seq_len - 1)
    else:
        phases = lax.rem(lag * seed[...], seq_len)
    angles = phases.astype(jnp.float32).T * (2.0 * math.pi / seq_len)
    features = jnp.concatenate([jnp.cos(angles), jnp.sin(angles)], axis=0)
    dims = (((0,), (0,)), ((), ()))
    exact = dict(precision=lax.Precision.HIGHEST, preferred_element_type=jnp.float32)
    shift = jnp.broadcast_to(bias[...], (8, bias.shape[1])).T[:, :1]
    hidden = jnp.sin(lax.dot_general(f_in[...], features, dims, **exact) + shift)
    shaped = lax.dot_general(hidden, f_out[...], dims, **exact)
    envelope = jnp.exp(-decay[...] * lag.astype(jnp.float32)) * scale
    taps = jnp.where(lag < reach[...] * block, shaped * envelope, 0.0).astype(jnp.bfloat16).T
    spectrum[...] = jnp.dot(taps, table[:lags], preferred_element_type=jnp.float32) + jnp.dot(
        taps, table[window : window + lags], preferred_element_type=jnp.float32
    )
    for copy in copies[7:]:
        copy.wait()


def transform(window, places, offsets, xs, valid, table, start, tile):
    block = xs[0].shape[1]
    blocks, factors = [], []
    for offset, x, there in zip(offsets, xs, valid):
        rows = x[offset + start : offset + start + tile]
        blocks.append(rows if there is None else jnp.where(there, rows, jnp.zeros_like(rows)))
    for base in (0, window):
        factors += [table[base + place * block : base + (place + 1) * block] for place in places]
    return jnp.dot(
        jnp.concatenate(blocks + blocks, axis=1),
        jnp.concatenate(factors, axis=0),
        preferred_element_type=jnp.float32,
    )


def block_there(window, block, place):
    back = window // block - 1 - place
    return None if back == 0 else lax.axis_index("seq") >= back


def respond(freq, group, per_group, window, spectrum, table):
    half = table.shape[1] // 2
    mult = []
    for g in range(freq.shape[0] // per_group):
        part = freq[g * per_group : (g + 1) * per_group]
        hc, hs = spectrum[group + g : group + g + 1, :half], spectrum[group + g : group + g + 1, half:]
        xc, xs = part[:, :half], part[:, half:]
        mult.append(jnp.concatenate([xc * hc - xs * hs, xc * hs + xs * hc], axis=1).astype(jnp.bfloat16))
    both = lax.dot_general(
        jnp.concatenate(mult, axis=0),
        table[2 * window :],
        (((1,), (1,)), ((), ())),
        preferred_element_type=jnp.float32,
    )
    block = both.shape[1] // 2
    return both[:, :block] + both[:, block:]


def tiles_of(channels):
    return [(start, min(256, channels - start)) for start in range(0, channels, 256)]


def ahead_kernel(window, per_group, first, own, other, spectrum, table, out):
    even = lax.axis_index("seq") % 2 == 0
    for start, tile in tiles_of(out.shape[0]):
        freq = transform(window, (0, 1), (0, 0), (own, other), (None, even), table, start, tile)
        ahead = respond(freq, (first + start) // per_group, per_group, window, spectrum, table)
        out[start : start + tile] = ahead.astype(out.dtype)


def gains(skip, row, block):
    gain = jnp.broadcast_to(skip[row : row + 1], (128, 128)).T
    return gain if block == 128 else jnp.broadcast_to(gain[:, :1], (128, block))


def base_kernel(window, places, odd_only, per_group, first, *refs):
    xs, (skip, spectrum, table, out) = refs[: len(places)], refs[len(places) :]
    block = out.shape[1]
    odd = lax.axis_index("seq") % 2 == 1
    valid = [odd if odd_only else block_there(window, block, place) for place in places[:-1]] + [None]
    for start, tile in tiles_of(out.shape[0]):
        freq = transform(window, places, [0] * len(xs), xs, valid, table, start, tile)
        mixed = respond(freq, (first + start) // per_group, per_group, window, spectrum, table)
        for low in range(0, tile, 128):
            here = slice(start + low, start + low + 128)
            gain = gains(skip, (first + start + low) // 128, block)
            out[here] = mixed[low : low + 128] + gain * xs[-1][here].astype(jnp.float32)


def last_kernel(first, carried, base, query, weight, before, part, gated_t):
    there = column_halves(weight)[1]
    arrived = lax.axis_index("seq") >= 2
    for start, tile in tiles_of(base.shape[0]):
        rows = slice(start, start + tile)
        mixed = base[rows] + jnp.where(arrived, carried[rows].astype(jnp.float32), 0.0)
        gated = query[first + start : first + start + tile].astype(jnp.float32) * mixed
        gated_t[:, rows] = gated.astype(jnp.bfloat16).T
    total = jnp.dot(gated_t[...], weight[first:, there], preferred_element_type=jnp.float32)
    part[...] = (before[...] + total).astype(part.dtype)


def column_halves(weight):
    cols = weight.shape[1] // 2
    core = lax.axis_index("chan")
    return [pl.ds(pl.multiple_of(part * cols, 128), cols) for part in (core, 1 - core)]


def hand_kernel(far, own, out):
    out[...] = jnp.where(lax.axis_index("seq") % 2 == 1, far[...], own[...])


def part_kernel(window, places, per_group, first, is_first, *refs):
    xs, refs = refs[: len(places)], refs[len(places) :]
    (base, query, spectrum, table, weight), refs = refs[:5], refs[5:]
    part, gated_t = refs[-2:]
    block, channels = gated_t.shape
    seq = lax.axis_index("seq")
    valid = [block_there(window, block, place) for place in places]

    def gate(start, tile, mixed):
        gated = query[first + start : first + start + tile].astype(jnp.float32) * mixed
        gated_t[:, start : start + tile] = gated.astype(jnp.bfloat16).T

    @pl.when(seq > 0)
    def _():
        for start, tile in tiles_of(channels):
            freq = transform(window, places, [0] * len(xs), xs, valid, table, start, tile)
            mixed = respond(freq, (first + start) // per_group, per_group, window, spectrum, table)
            gate(start, tile, base[start : start + tile] + mixed)

    @pl.when(seq == 0)
    def _():
        for start, tile in tiles_of(channels):
            gate(start, tile, base[start : start + tile])

    there = column_halves(weight)[1]
    total = jnp.dot(gated_t[...], weight[first : first + channels, there], preferred_element_type=jnp.float32)
    if not is_first:
        total = refs[0][...] + total
    part[...] = total.astype(part.dtype)


def own_kernel(gated_a, gated_b, weight, out):
    here = column_halves(weight)[0]
    gated_t = jnp.concatenate([gated_a[...], gated_b[...]], axis=1)
    out[...] = jnp.dot(gated_t, weight[:, here], preferred_element_type=jnp.float32)


def cost(bytes_accessed):
    return pl.CostEstimate(flops=1, bytes_accessed=bytes_accessed, transcendentals=0)


def shift(array, back, cyclic):
    count = lax.axis_size("seq")
    return lax.ppermute(array, "seq", [(i, (i + back) % count) for i in range(count if cyclic else count - back)])


def swap_pairs(array):
    return lax.ppermute(array, "seq", [(i, i ^ 1) for i in range(lax.axis_size("seq"))])


def body(
    query_feat,
    key_feat,
    value_feat,
    filter_seed,
    filter_in,
    filter_bias,
    filter_out,
    decay_rate,
    reach_blocks,
    skip_gain,
    out_weight,
):
    channels, block = query_feat.shape
    seq_count = lax.axis_size("seq")
    reach_max = seq_count // 4
    filters = decay_rate.shape[0]
    per_group = channels // filters
    lags = reach_max * block
    window = lags + block
    (fwd_hi, fwd_lo), (inv_hi, inv_lo) = transform_tables(window, lags, block)
    table = np.concatenate([fwd_hi, fwd_lo, inv_hi.T, inv_lo.T], axis=0)
    length = table.shape[1]
    out_cols = out_weight.shape[1]
    cols = out_cols // 2
    params = pltpu.CompilerParams(vmem_limit_bytes=VMEM_BYTES)
    vmem = pl.BlockSpec(memory_space=pltpu.VMEM)
    f32, bf16 = jnp.float32, jnp.bfloat16
    shape = jax.ShapeDtypeStruct

    products = [
        (key_feat[low:high].astype(f32) * value_feat[low:high].astype(f32)).astype(bf16)
        for low, high in ((0, RELAYED), (RELAYED, channels))
    ]
    if reach_max == 2:
        other = swap_pairs(products[1])
        far = shift(products[0], 2, WRAP_FAR)

    small = (
        filter_seed[None],
        filter_in,
        filter_bias[None],
        filter_out,
        decay_rate[None],
        reach_blocks[None],
    )
    large = (
        jnp.asarray(table),
        query_feat,
        skip_gain.reshape(-1, 128),
    )
    weight_in = pltpu.with_memory_space_constraint(out_weight, pltpu.HBM)
    spectrum, table, query, skip, weight = pl.pallas_call(
        lambda *refs: setup_kernel(block * seq_count, block, 1.0 / math.sqrt(lags), *refs),
        in_specs=[pl.BlockSpec(memory_space=pltpu.HBM)] * 10,
        out_specs=[vmem] * 5,
        out_shape=[pltpu.VMEM((filters, length), f32)] + [pltpu.VMEM(a.shape, a.dtype) for a in large]
        + [pltpu.VMEM(out_weight.shape, bf16)],
        scratch_shapes=[pltpu.VMEM(a.shape, a.dtype) for a in small] + [pltpu.SemaphoreType.DMA((10,))],
        compiler_params=params,
        cost_estimate=cost(SETUP_COST),
    )(*[pltpu.with_memory_space_constraint(a, pltpu.HBM) for a in small + large], weight_in)

    def kernel(call, ins, *outs):
        return pl.pallas_call(
            call,
            in_specs=[vmem] * len(ins),
            out_specs=[vmem] * len(outs),
            out_shape=outs,
            compiler_params=params,
            cost_estimate=cost(TAIL_COST),
        )(*ins)

    def base(first, blocks, odd_only=False):
        call = functools.partial(base_kernel, window, tuple(blocks), odd_only, per_group, first)
        return kernel(call, (*blocks.values(), skip, spectrum, table), shape(blocks[reach_max].shape, f32))[0]

    def part(first, late, early, sums, dtype):
        ins = (*late.values(), early, query, spectrum, table, weight, *sums)
        call = functools.partial(part_kernel, window, tuple(late), per_group, first, not sums)
        return kernel(call, ins, shape((block, cols), dtype), shape((block, early.shape[0]), bf16))

    own_a, own_b = products
    if reach_max == 2:
        (sent,) = kernel(
            functools.partial(ahead_kernel, window, per_group, RELAYED),
            (own_b, other, spectrum, table),
            shape(own_b.shape, bf16),
        )
        carried = shift(sent, 2, WRAP_SENT)
        ready, _ = lax.optimization_barrier((own_a, sent))
        (handed,) = kernel(hand_kernel, (far, ready), shape(own_a.shape, bf16))
        near = swap_pairs(handed)
        base_a = base(0, {0: far, 2: own_a})
        base_b = base(RELAYED, {1: other, 2: own_b}, True)
        sums, gated_a = part(0, {1: near}, base_a, (), f32)
        sums, gated_b = kernel(
            functools.partial(last_kernel, RELAYED),
            (carried, base_b, query, weight, sums),
            shape((block, cols), bf16),
            shape((block, channels - RELAYED), bf16),
        )
    else:
        halos = [{reach_max - back: shift(own, back, False) for back in range(1, reach_max + 1)} for own in products]
        sums, gated_a = part(0, halos[0], base(0, {reach_max: own_a}), (), f32)
        sums, gated_b = part(RELAYED, halos[1], base(RELAYED, {reach_max: own_b}), (sums,), bf16)
    received = lax.ppermute(sums, "chan", [(0, 1), (1, 0)])
    (own,) = kernel(own_kernel, (gated_a, gated_b, weight), shape((block, cols), f32))
    return (own + received.astype(f32)).astype(bf16)


def solution(mesh):
    return jax.shard_map(
        body,
        mesh=mesh,
        in_specs=(
            P("chan", ("groups", "seq")),
            P("chan", ("groups", "seq")),
            P("chan", ("groups", "seq")),
            P(),
            P(),
            P(),
            P(None, "chan"),
            P("chan"),
            P("chan"),
            P("chan"),
            P("chan", None),
        ),
        out_specs=P(("groups", "seq"), "chan"),
        check_vma=False,
    )
```

```python
import functools
import math

import jax
import jax.numpy as jnp
import numpy as np
from jax import lax
from jax.experimental import pallas as pl
from jax.experimental.pallas import tpu as pltpu
from jax.sharding import PartitionSpec as P

SETUP_COST = 30_000_000
TAIL_COST = 1
VMEM_BYTES = 24 * 1024 * 1024
RELAYED = 1024
TILE = 256
WRAP_FAR = True
WRAP_SENT = False


def split_bf16(array):
    high = array.astype(jnp.bfloat16)
    low = (array - high.astype(np.float64)).astype(jnp.bfloat16)
    return high, low


def transform_tables(window, first_out, block):
    half = 128 * math.ceil(window / 256)
    omega = (np.arange(half) + 0.5) * (math.pi / half)
    angle = np.arange(window)[:, None] * omega[None, :]
    forward = np.concatenate([np.cos(angle), np.sin(angle)], axis=1)
    back = omega[:, None] * (first_out + np.arange(block))[None, :]
    inverse = np.concatenate([np.cos(back), np.sin(back)], axis=0) / half
    return split_bf16(forward), split_bf16(inverse)


def setup_kernel(seq_len, block, scale, *refs):
    small, weight, spectrum, weight_out, local, sems = refs[:6], refs[9], refs[10], refs[14], refs[15:21], refs[21]
    table = refs[11]
    pairs = list(zip(small, local)) + list(zip(refs[6:9], refs[11:14]))
    pairs.append((weight, weight_out))
    copies = [pltpu.make_async_copy(source, target, sems.at[k]) for k, (source, target) in enumerate(pairs)]
    for copy in copies:
        copy.start()
    for copy in copies[:7]:
        copy.wait()
    seed, f_in, bias, f_out, decay, reach = local
    window = (table.shape[0] - block) // 2
    lags = window - block
    lag = lax.broadcasted_iota(jnp.int32, (lags, 1), 0)
    if seq_len & (seq_len - 1) == 0:
        phases = (lag * seed[...]) & (seq_len - 1)
    else:
        phases = lax.rem(lag * seed[...], seq_len)
    angles = phases.astype(jnp.float32).T * (2.0 * math.pi / seq_len)
    features = jnp.concatenate([jnp.cos(angles), jnp.sin(angles)], axis=0)
    dims = (((0,), (0,)), ((), ()))
    exact = dict(precision=lax.Precision.HIGHEST, preferred_element_type=jnp.float32)
    shift = jnp.broadcast_to(bias[...], (8, bias.shape[1])).T[:, :1]
    hidden = jnp.sin(lax.dot_general(f_in[...], features, dims, **exact) + shift)
    shaped = lax.dot_general(hidden, f_out[...], dims, **exact)
    envelope = jnp.exp(-decay[...] * lag.astype(jnp.float32)) * scale
    taps = jnp.where(lag < reach[...] * block, shaped * envelope, 0.0).astype(jnp.bfloat16).T
    spectrum[...] = jnp.dot(taps, table[:lags], preferred_element_type=jnp.float32) + jnp.dot(
        taps, table[window : window + lags], preferred_element_type=jnp.float32
    )
    for copy in copies[7:]:
        copy.wait()


def transform(places, xs, valid, table, start, tile):
    block = xs[0].shape[1]
    blocks = []
    for x, there in zip(xs, valid):
        rows = x[start : start + tile]
        blocks.append(rows if there is None else jnp.where(there, rows, jnp.zeros_like(rows)))
    factors = [table[place * block : (place + 1) * block] for place in places]
    return jnp.dot(
        jnp.concatenate(blocks, axis=1), jnp.concatenate(factors, axis=0), preferred_element_type=jnp.float32
    )


def block_there(window, block, place):
    back = window // block - 1 - place
    return None if back == 0 else lax.axis_index("seq") >= back


def respond(freq, group, per_group, window, spectrum, table):
    half = table.shape[1] // 2
    mult = []
    for g in range(freq.shape[0] // per_group):
        part = freq[g * per_group : (g + 1) * per_group]
        hc, hs = spectrum[group + g : group + g + 1, :half], spectrum[group + g : group + g + 1, half:]
        xc, xs = part[:, :half], part[:, half:]
        mult.append(jnp.concatenate([xc * hc - xs * hs, xc * hs + xs * hc], axis=1).astype(jnp.bfloat16))
    block = table.shape[0] - 2 * window
    both = lax.dot_general(
        jnp.concatenate(mult, axis=0),
        table[2 * window - block :],
        (((1,), (1,)), ((), ())),
        preferred_element_type=jnp.float32,
    )
    return both[:, :block] + both[:, block:]


def in_stages(channels, first, second):
    tiles = [(start, min(TILE, channels - start)) for start in range(0, channels, TILE)]
    ready = first(*tiles[0])
    for k, tile in enumerate(tiles):
        now = ready
        if k + 1 < len(tiles):
            ready = first(*tiles[k + 1])
        second(*tile, now)


def ahead_kernel(window, per_group, first, own, other, spectrum, table, out):
    even = lax.axis_index("seq") % 2 == 0

    def give(start, tile, freq):
        ahead = respond(freq, (first + start) // per_group, per_group, window, spectrum, table)
        out[start : start + tile] = ahead.astype(out.dtype)

    in_stages(out.shape[0], functools.partial(transform, (0, 1), (own, other), (None, even), table), give)


def gains(skip, row, block):
    gain = jnp.broadcast_to(skip[row : row + 1], (128, 128)).T
    return gain if block == 128 else jnp.broadcast_to(gain[:, :1], (128, block))


def base_kernel(window, places, odd_only, per_group, first, *refs):
    xs, (skip, spectrum, table, out) = refs[: len(places)], refs[len(places) :]
    block = out.shape[1]
    odd = lax.axis_index("seq") % 2 == 1
    valid = [odd if odd_only else block_there(window, block, place) for place in places[:-1]] + [None]

    def give(start, tile, freq):
        mixed = respond(freq, (first + start) // per_group, per_group, window, spectrum, table)
        for low in range(0, tile, 128):
            here = slice(start + low, start + low + 128)
            gain = gains(skip, (first + start + low) // 128, block)
            out[here] = mixed[low : low + 128] + gain * xs[-1][here].astype(jnp.float32)

    in_stages(out.shape[0], functools.partial(transform, places, xs, valid, table), give)


def last_kernel(first, carried, base, query, weight, before, part, gated_t):
    there = column_halves(weight)[1]
    arrived = lax.axis_index("seq") >= 2
    for start in range(0, base.shape[0], 128):
        rows = slice(start, start + 128)
        mixed = base[rows] + jnp.where(arrived, carried[rows].astype(jnp.float32), 0.0)
        gated = query[first + start : first + start + 128].astype(jnp.float32) * mixed
        gated_t[:, rows] = gated.astype(jnp.bfloat16).T
    total = jnp.dot(gated_t[...], weight[first:, there], preferred_element_type=jnp.float32)
    part[...] = (before[...] + total).astype(part.dtype)


def column_halves(weight):
    cols = weight.shape[1] // 2
    core = lax.axis_index("chan")
    return [pl.ds(pl.multiple_of(part * cols, 128), cols) for part in (core, 1 - core)]


def hand_kernel(far, own, out):
    out[...] = jnp.where(lax.axis_index("seq") % 2 == 1, far[...], own[...])


def part_kernel(window, places, per_group, first, is_first, *refs):
    xs, refs = refs[: len(places)], refs[len(places) :]
    (base, query, spectrum, table, weight), refs = refs[:5], refs[5:]
    part, gated_t = refs[-2:]
    block, channels = gated_t.shape
    seq = lax.axis_index("seq")
    valid = [block_there(window, block, place) for place in places]

    def gate(start, tile, mixed):
        gated = query[first + start : first + start + tile].astype(jnp.float32) * mixed
        gated_t[:, start : start + tile] = gated.astype(jnp.bfloat16).T

    def add(start, tile, freq):
        mixed = respond(freq, (first + start) // per_group, per_group, window, spectrum, table)
        gate(start, tile, base[start : start + tile] + mixed)

    @pl.when(seq > 0)
    def _():
        in_stages(channels, functools.partial(transform, places, xs, valid, table), add)

    @pl.when(seq == 0)
    def _():
        for start in range(0, channels, 128):
            gate(start, 128, base[start : start + 128])

    there = column_halves(weight)[1]
    total = jnp.dot(gated_t[...], weight[first : first + channels, there], preferred_element_type=jnp.float32)
    if not is_first:
        total = refs[0][...] + total
    part[...] = total.astype(part.dtype)


def own_kernel(gated_a, gated_b, weight, out):
    here = column_halves(weight)[0]
    gated_t = jnp.concatenate([gated_a[...], gated_b[...]], axis=1)
    out[...] = jnp.dot(gated_t, weight[:, here], preferred_element_type=jnp.float32)


def cost(bytes_accessed):
    return pl.CostEstimate(flops=1, bytes_accessed=bytes_accessed, transcendentals=0)


def shift(array, back, cyclic):
    count = lax.axis_size("seq")
    return lax.ppermute(array, "seq", [(i, (i + back) % count) for i in range(count if cyclic else count - back)])


def swap_pairs(array):
    return lax.ppermute(array, "seq", [(i, i ^ 1) for i in range(lax.axis_size("seq"))])


def body(
    query_feat,
    key_feat,
    value_feat,
    filter_seed,
    filter_in,
    filter_bias,
    filter_out,
    decay_rate,
    reach_blocks,
    skip_gain,
    out_weight,
):
    channels, block = query_feat.shape
    seq_count = lax.axis_size("seq")
    reach_max = seq_count // 4
    filters = decay_rate.shape[0]
    per_group = channels // filters
    lags = reach_max * block
    window = lags + block
    (fwd_hi, fwd_lo), (inv_hi, inv_lo) = transform_tables(window, lags, block)
    table = np.concatenate([fwd_hi, fwd_lo[:lags], inv_hi.T, inv_lo.T], axis=0)
    length = table.shape[1]
    out_cols = out_weight.shape[1]
    cols = out_cols // 2
    params = pltpu.CompilerParams(vmem_limit_bytes=VMEM_BYTES)
    vmem = pl.BlockSpec(memory_space=pltpu.VMEM)
    f32, bf16 = jnp.float32, jnp.bfloat16
    shape = jax.ShapeDtypeStruct

    products = [
        (key_feat[low:high].astype(f32) * value_feat[low:high].astype(f32)).astype(bf16)
        for low, high in ((0, RELAYED), (RELAYED, channels))
    ]
    if reach_max == 2:
        other = swap_pairs(products[1])
        far = shift(products[0], 2, WRAP_FAR)

    small = (
        filter_seed[None],
        filter_in,
        filter_bias[None],
        filter_out,
        decay_rate[None],
        reach_blocks[None],
    )
    large = (
        jnp.asarray(table),
        query_feat,
        skip_gain.reshape(-1, 128),
    )
    weight_in = pltpu.with_memory_space_constraint(out_weight, pltpu.HBM)
    spectrum, table, query, skip, weight = pl.pallas_call(
        lambda *refs: setup_kernel(block * seq_count, block, 1.0 / math.sqrt(lags), *refs),
        in_specs=[pl.BlockSpec(memory_space=pltpu.HBM)] * 10,
        out_specs=[vmem] * 5,
        out_shape=[pltpu.VMEM((filters, length), f32)] + [pltpu.VMEM(a.shape, a.dtype) for a in large]
        + [pltpu.VMEM(out_weight.shape, bf16)],
        scratch_shapes=[pltpu.VMEM(a.shape, a.dtype) for a in small] + [pltpu.SemaphoreType.DMA((10,))],
        compiler_params=params,
        cost_estimate=cost(SETUP_COST),
    )(*[pltpu.with_memory_space_constraint(a, pltpu.HBM) for a in small + large], weight_in)

    def kernel(call, ins, *outs):
        return pl.pallas_call(
            call,
            in_specs=[vmem] * len(ins),
            out_specs=[vmem] * len(outs),
            out_shape=outs,
            compiler_params=params,
            cost_estimate=cost(TAIL_COST),
        )(*ins)

    def base(first, blocks, odd_only=False):
        call = functools.partial(base_kernel, window, tuple(blocks), odd_only, per_group, first)
        return kernel(call, (*blocks.values(), skip, spectrum, table), shape(blocks[reach_max].shape, f32))[0]

    def part(first, late, early, sums, dtype):
        ins = (*late.values(), early, query, spectrum, table, weight, *sums)
        call = functools.partial(part_kernel, window, tuple(late), per_group, first, not sums)
        return kernel(call, ins, shape((block, cols), dtype), shape((block, early.shape[0]), bf16))

    own_a, own_b = products
    if reach_max == 2:
        (sent,) = kernel(
            functools.partial(ahead_kernel, window, per_group, RELAYED),
            (own_b, other, spectrum, table),
            shape(own_b.shape, bf16),
        )
        carried = shift(sent, 2, WRAP_SENT)
        ready, _ = lax.optimization_barrier((own_a, spectrum))
        (handed,) = kernel(hand_kernel, (far, ready), shape(own_a.shape, bf16))
        near = swap_pairs(handed)
        base_a = base(0, {0: far, 2: own_a})
        base_b = base(RELAYED, {1: other, 2: own_b}, True)
        sums, gated_a = part(0, {1: near}, base_a, (), f32)
        sums, gated_b = kernel(
            functools.partial(last_kernel, RELAYED),
            (carried, base_b, query, weight, sums),
            shape((block, cols), bf16),
            shape((block, channels - RELAYED), bf16),
        )
    else:
        halos = [{reach_max - back: shift(own, back, False) for back in range(1, reach_max + 1)} for own in products]
        sums, gated_a = part(0, halos[0], base(0, {reach_max: own_a}), (), f32)
        sums, gated_b = part(RELAYED, halos[1], base(RELAYED, {reach_max: own_b}), (sums,), bf16)
    received = lax.ppermute(sums, "chan", [(0, 1), (1, 0)])
    (own,) = kernel(own_kernel, (gated_a, gated_b, weight), shape((block, cols), f32))
    return (own + received.astype(f32)).astype(bf16)


def solution(mesh):
    return jax.shard_map(
        body,
        mesh=mesh,
        in_specs=(
            P("chan", ("groups", "seq")),
            P("chan", ("groups", "seq")),
            P("chan", ("groups", "seq")),
            P(),
            P(),
            P(),
            P(None, "chan"),
            P("chan"),
            P("chan"),
            P("chan"),
            P("chan", None),
        ),
        out_specs=P(("groups", "seq"), "chan"),
        check_vma=False,
    )
```

```python
import functools
import math

import jax
import jax.numpy as jnp
import numpy as np
from jax import lax
from jax.experimental import pallas as pl
from jax.experimental.pallas import tpu as pltpu
from jax.sharding import PartitionSpec as P

SETUP_COST = 30_000_000
TAIL_COST = 1
VMEM_BYTES = 24 * 1024 * 1024
RELAYED = 1024
TILE = 512
WRAP_FAR = True
WRAP_SENT = False


def split_bf16(array):
    high = array.astype(jnp.bfloat16)
    low = (array - high.astype(np.float64)).astype(jnp.bfloat16)
    return high, low


def transform_tables(window, first_out, block):
    half = 128 * math.ceil(window / 256)
    omega = (np.arange(half) + 0.5) * (math.pi / half)
    angle = np.arange(window)[:, None] * omega[None, :]
    forward = np.concatenate([np.cos(angle), np.sin(angle)], axis=1)
    back = omega[:, None] * (first_out + np.arange(block))[None, :]
    inverse = np.concatenate([np.cos(back), np.sin(back)], axis=0) / half
    return split_bf16(forward), split_bf16(inverse)


def setup_kernel(seq_len, block, scale, *refs):
    small, weight, spectrum, weight_out, local, sems = refs[:6], refs[9], refs[10], refs[14], refs[15:21], refs[21]
    table = refs[11]
    pairs = list(zip(small, local)) + list(zip(refs[6:9], refs[11:14]))
    pairs.append((weight, weight_out))
    copies = [pltpu.make_async_copy(source, target, sems.at[k]) for k, (source, target) in enumerate(pairs)]
    for copy in copies:
        copy.start()
    for copy in copies[:7]:
        copy.wait()
    seed, f_in, bias, f_out, decay, reach = local
    window = (table.shape[0] - block) // 2
    lags = window - block
    lag = lax.broadcasted_iota(jnp.int32, (lags, 1), 0)
    if seq_len & (seq_len - 1) == 0:
        phases = (lag * seed[...]) & (seq_len - 1)
    else:
        phases = lax.rem(lag * seed[...], seq_len)
    angles = phases.astype(jnp.float32).T * (2.0 * math.pi / seq_len)
    features = jnp.concatenate([jnp.cos(angles), jnp.sin(angles)], axis=0)
    dims = (((0,), (0,)), ((), ()))
    exact = dict(precision=lax.Precision.HIGHEST, preferred_element_type=jnp.float32)
    shift = jnp.broadcast_to(bias[...], (8, bias.shape[1])).T[:, :1]
    hidden = jnp.sin(lax.dot_general(f_in[...], features, dims, **exact) + shift)
    shaped = lax.dot_general(hidden, f_out[...], dims, **exact)
    envelope = jnp.exp(-decay[...] * lag.astype(jnp.float32)) * scale
    taps = jnp.where(lag < reach[...] * block, shaped * envelope, 0.0).astype(jnp.bfloat16).T
    spectrum[...] = jnp.dot(taps, table[:lags], preferred_element_type=jnp.float32) + jnp.dot(
        taps, table[window : window + lags], preferred_element_type=jnp.float32
    )
    for copy in copies[7:]:
        copy.wait()


def transform(places, xs, valid, table, start, tile):
    block = xs[0].shape[1]
    blocks = []
    for x, there in zip(xs, valid):
        rows = x[start : start + tile]
        blocks.append(rows if there is None else jnp.where(there, rows, jnp.zeros_like(rows)))
    factors = [table[place * block : (place + 1) * block] for place in places]
    return jnp.dot(
        jnp.concatenate(blocks, axis=1), jnp.concatenate(factors, axis=0), preferred_element_type=jnp.float32
    )


def block_there(window, block, place):
    back = window // block - 1 - place
    return None if back == 0 else lax.axis_index("seq") >= back


def respond(freq, group, per_group, window, spectrum, table):
    half = table.shape[1] // 2
    mult = []
    for g in range(freq.shape[0] // per_group):
        part = freq[g * per_group : (g + 1) * per_group]
        hc, hs = spectrum[group + g : group + g + 1, :half], spectrum[group + g : group + g + 1, half:]
        xc, xs = part[:, :half], part[:, half:]
        mult.append(jnp.concatenate([xc * hc - xs * hs, xc * hs + xs * hc], axis=1).astype(jnp.bfloat16))
    block = table.shape[0] - 2 * window
    both = lax.dot_general(
        jnp.concatenate(mult, axis=0),
        table[2 * window - block :],
        (((1,), (1,)), ((), ())),
        preferred_element_type=jnp.float32,
    )
    return both[:, :block] + both[:, block:]


def in_stages(channels, first, second):
    tiles = [(start, min(TILE, channels - start)) for start in range(0, channels, TILE)]
    ready = first(*tiles[0])
    for k, tile in enumerate(tiles):
        now = ready
        if k + 1 < len(tiles):
            ready = first(*tiles[k + 1])
        second(*tile, now)


def ahead_kernel(window, per_group, first, own, other, spectrum, table, out):
    even = lax.axis_index("seq") % 2 == 0

    def give(start, tile, freq):
        ahead = respond(freq, (first + start) // per_group, per_group, window, spectrum, table)
        out[start : start + tile] = ahead.astype(out.dtype)

    in_stages(out.shape[0], functools.partial(transform, (0, 1), (own, other), (None, even), table), give)


def gains(skip, row, block):
    gain = jnp.broadcast_to(skip[row : row + 1], (128, 128)).T
    return gain if block == 128 else jnp.broadcast_to(gain[:, :1], (128, block))


def base_kernel(window, places, odd_only, per_group, first, *refs):
    xs, (skip, spectrum, table, out) = refs[: len(places)], refs[len(places) :]
    block = out.shape[1]
    odd = lax.axis_index("seq") % 2 == 1
    valid = [odd if odd_only else block_there(window, block, place) for place in places[:-1]] + [None]

    def give(start, tile, freq):
        mixed = respond(freq, (first + start) // per_group, per_group, window, spectrum, table)
        for low in range(0, tile, 128):
            here = slice(start + low, start + low + 128)
            gain = gains(skip, (first + start + low) // 128, block)
            out[here] = mixed[low : low + 128] + gain * xs[-1][here].astype(jnp.float32)

    in_stages(out.shape[0], functools.partial(transform, places, xs, valid, table), give)


def column_halves(weight):
    cols = weight.shape[1] // 2
    core = lax.axis_index("chan")
    return [pl.ds(pl.multiple_of(part * cols, 128), cols) for part in (core, 1 - core)]


def gate(first, query, gated_t, start, mixed):
    rows = slice(start, start + mixed.shape[0])
    gated = query[first + start : first + start + mixed.shape[0]].astype(jnp.float32) * mixed
    gated_t[:, rows] = gated.astype(jnp.bfloat16).T


def first_block_kernel(splits, base_a, base_b, query, weight, gated_a, gated_b, part):
    there = column_halves(weight)[1]

    @pl.when(lax.axis_index("seq") == 0)
    def _():
        total = 0.0
        for first, base, gated_t in zip(splits, (base_a, base_b), (gated_a, gated_b)):
            channels = base.shape[0]
            for start in range(0, channels, 128):
                gate(first, query, gated_t, start, base[start : start + 128])
            total += jnp.dot(
                gated_t[...], weight[first : first + channels, there], preferred_element_type=jnp.float32
            )
        part[...] = total.astype(part.dtype)


def last_kernel(first, carried, base, query, weight, before, gated_in, part_in, gated_t, part):
    there = column_halves(weight)[1]
    seq = lax.axis_index("seq")

    @pl.when(seq > 0)
    def _():
        for start in range(0, base.shape[0], 128):
            rows = slice(start, start + 128)
            gate(first, query, gated_t, start, base[rows] + jnp.where(seq >= 2, carried[rows].astype(jnp.float32), 0.0))
        total = jnp.dot(gated_t[...], weight[first:, there], preferred_element_type=jnp.float32)
        part[...] = (before[...] + total).astype(part.dtype)


def hand_kernel(far, own, out):
    out[...] = jnp.where(lax.axis_index("seq") % 2 == 1, far[...], own[...])


def part_kernel(window, places, per_group, first, is_first, *refs):
    xs, refs = refs[: len(places)], refs[len(places) :]
    (base, query, spectrum, table, weight), refs = refs[:5], refs[5:]
    gated_t, part = refs[-2:]
    block, channels = gated_t.shape
    seq = lax.axis_index("seq")
    valid = [block_there(window, block, place) for place in places]
    there = column_halves(weight)[1]

    def add(start, tile, freq):
        mixed = respond(freq, (first + start) // per_group, per_group, window, spectrum, table)
        gate(first, query, gated_t, start, base[start : start + tile] + mixed)

    @pl.when(seq > 0)
    def _():
        in_stages(channels, functools.partial(transform, places, xs, valid, table), add)
        total = jnp.dot(gated_t[...], weight[first : first + channels, there], preferred_element_type=jnp.float32)
        if not is_first:
            total = refs[0][...] + total
        part[...] = total.astype(part.dtype)


def own_kernel(gated_a, gated_b, weight, out):
    here = column_halves(weight)[0]
    gated_t = jnp.concatenate([gated_a[...], gated_b[...]], axis=1)
    out[...] = jnp.dot(gated_t, weight[:, here], preferred_element_type=jnp.float32)


def cost(bytes_accessed):
    return pl.CostEstimate(flops=1, bytes_accessed=bytes_accessed, transcendentals=0)


def shift(array, back, cyclic):
    count = lax.axis_size("seq")
    return lax.ppermute(array, "seq", [(i, (i + back) % count) for i in range(count if cyclic else count - back)])


def swap_pairs(array):
    return lax.ppermute(array, "seq", [(i, i ^ 1) for i in range(lax.axis_size("seq"))])


def body(
    query_feat,
    key_feat,
    value_feat,
    filter_seed,
    filter_in,
    filter_bias,
    filter_out,
    decay_rate,
    reach_blocks,
    skip_gain,
    out_weight,
):
    channels, block = query_feat.shape
    seq_count = lax.axis_size("seq")
    reach_max = seq_count // 4
    filters = decay_rate.shape[0]
    per_group = channels // filters
    lags = reach_max * block
    window = lags + block
    (fwd_hi, fwd_lo), (inv_hi, inv_lo) = transform_tables(window, lags, block)
    table = np.concatenate([fwd_hi, fwd_lo[:lags], inv_hi.T, inv_lo.T], axis=0)
    length = table.shape[1]
    out_cols = out_weight.shape[1]
    cols = out_cols // 2
    params = pltpu.CompilerParams(vmem_limit_bytes=VMEM_BYTES)
    vmem = pl.BlockSpec(memory_space=pltpu.VMEM)
    f32, bf16 = jnp.float32, jnp.bfloat16
    shape = jax.ShapeDtypeStruct

    products = [
        (key_feat[low:high].astype(f32) * value_feat[low:high].astype(f32)).astype(bf16)
        for low, high in ((0, RELAYED), (RELAYED, channels))
    ]
    if reach_max == 2:
        other = swap_pairs(products[1])
        far = shift(products[0], 2, WRAP_FAR)

    small = (
        filter_seed[None],
        filter_in,
        filter_bias[None],
        filter_out,
        decay_rate[None],
        reach_blocks[None],
    )
    large = (
        jnp.asarray(table),
        query_feat,
        skip_gain.reshape(-1, 128),
    )
    weight_in = pltpu.with_memory_space_constraint(out_weight, pltpu.HBM)
    spectrum, table, query, skip, weight = pl.pallas_call(
        lambda *refs: setup_kernel(block * seq_count, block, 1.0 / math.sqrt(lags), *refs),
        in_specs=[pl.BlockSpec(memory_space=pltpu.HBM)] * 10,
        out_specs=[vmem] * 5,
        out_shape=[pltpu.VMEM((filters, length), f32)] + [pltpu.VMEM(a.shape, a.dtype) for a in large]
        + [pltpu.VMEM(out_weight.shape, bf16)],
        scratch_shapes=[pltpu.VMEM(a.shape, a.dtype) for a in small] + [pltpu.SemaphoreType.DMA((10,))],
        compiler_params=params,
        cost_estimate=cost(SETUP_COST),
    )(*[pltpu.with_memory_space_constraint(a, pltpu.HBM) for a in small + large], weight_in)

    def kernel(call, ins, *outs, aliases={}):
        return pl.pallas_call(
            call,
            in_specs=[vmem] * len(ins),
            out_specs=[vmem] * len(outs),
            out_shape=outs,
            input_output_aliases=aliases,
            compiler_params=params,
            cost_estimate=cost(TAIL_COST),
        )(*ins)

    def base(first, blocks, odd_only=False):
        call = functools.partial(base_kernel, window, tuple(blocks), odd_only, per_group, first)
        return kernel(call, (*blocks.values(), skip, spectrum, table), shape(blocks[reach_max].shape, f32))[0]

    def first_block(base_a, base_b):
        shapes = [shape((block, base.shape[0]), bf16) for base in (base_a, base_b)]
        call = functools.partial(first_block_kernel, (0, RELAYED))
        return kernel(call, (base_a, base_b, query, weight), *shapes, shape((block, cols), bf16))

    def part(first, late, early, sums, gated, total=None):
        ins = (*late.values(), early, query, spectrum, table, weight, *sums, gated)
        aliases = {len(ins) - 1: 0}
        outs = [shape(gated.shape, bf16), shape((block, cols), f32)]
        if total is not None:
            aliases[len(ins)] = 1
            ins, outs[1] = (*ins, total), shape(total.shape, bf16)
        call = functools.partial(part_kernel, window, tuple(late), per_group, first, not sums)
        return kernel(call, ins, *outs, aliases=aliases)

    own_a, own_b = products
    if reach_max == 2:
        (sent,) = kernel(
            functools.partial(ahead_kernel, window, per_group, RELAYED),
            (own_b, other, spectrum, table),
            shape(own_b.shape, bf16),
        )
        carried = shift(sent, 2, WRAP_SENT)
        ready, _ = lax.optimization_barrier((own_a, spectrum))
        (handed,) = kernel(hand_kernel, (far, ready), shape(own_a.shape, bf16))
        near = swap_pairs(handed)
        base_a = base(0, {0: far, 2: own_a})
        base_b = base(RELAYED, {1: other, 2: own_b}, True)
        gated_a, gated_b, sums_b = first_block(base_a, base_b)
        gated_a, sums_a = part(0, {1: near}, base_a, (), gated_a)
        gated_b, sums = kernel(
            functools.partial(last_kernel, RELAYED),
            (carried, base_b, query, weight, sums_a, gated_b, sums_b),
            shape(gated_b.shape, bf16),
            shape(sums_b.shape, bf16),
            aliases={5: 0, 6: 1},
        )
    else:
        halos = [{reach_max - back: shift(own, back, False) for back in range(1, reach_max + 1)} for own in products]
        base_a, base_b = base(0, {reach_max: own_a}), base(RELAYED, {reach_max: own_b})
        gated_a, gated_b, sums_b = first_block(base_a, base_b)
        gated_a, sums_a = part(0, halos[0], base_a, (), gated_a)
        gated_b, sums = part(RELAYED, halos[1], base_b, (sums_a,), gated_b, sums_b)
    received = lax.ppermute(sums, "chan", [(0, 1), (1, 0)])
    (own,) = kernel(own_kernel, (gated_a, gated_b, weight), shape((block, cols), f32))
    return (own + received.astype(f32)).astype(bf16)


def solution(mesh):
    return jax.shard_map(
        body,
        mesh=mesh,
        in_specs=(
            P("chan", ("groups", "seq")),
            P("chan", ("groups", "seq")),
            P("chan", ("groups", "seq")),
            P(),
            P(),
            P(),
            P(None, "chan"),
            P("chan"),
            P("chan"),
            P("chan"),
            P("chan", None),
        ),
        out_specs=P(("groups", "seq"), "chan"),
        check_vma=False,
    )
```

```python
import functools
import math

import jax
import jax.numpy as jnp
import numpy as np
from jax import lax
from jax.experimental import pallas as pl
from jax.experimental.pallas import tpu as pltpu
from jax.sharding import PartitionSpec as P

SETUP_COST = 30_000_000
TAIL_COST = 1
VMEM_BYTES = 24 * 1024 * 1024
RELAYED = 1024
TILE = 512
WRAP_FAR = True
WRAP_SENT = False


def split_bf16(array):
    high = array.astype(jnp.bfloat16)
    low = (array - high.astype(np.float64)).astype(jnp.bfloat16)
    return high, low


def transform_tables(window, first_out, block):
    half = 128 * math.ceil(window / 256)
    omega = (np.arange(half) + 0.5) * (math.pi / half)
    angle = np.arange(window)[:, None] * omega[None, :]
    forward = np.concatenate([np.cos(angle), np.sin(angle)], axis=1)
    back = omega[:, None] * (first_out + np.arange(block))[None, :]
    inverse = np.concatenate([np.cos(back), np.sin(back)], axis=0) / half
    return split_bf16(forward), split_bf16(inverse)


def setup_kernel(seq_len, block, scale, *refs):
    small, weight, spectrum, weight_out, local, sems = refs[:6], refs[9], refs[10], refs[14], refs[15:21], refs[21]
    table = refs[11]
    pairs = list(zip(small, local)) + list(zip(refs[6:9], refs[11:14]))
    pairs.append((weight, weight_out))
    copies = [pltpu.make_async_copy(source, target, sems.at[k]) for k, (source, target) in enumerate(pairs)]
    for copy in copies:
        copy.start()
    for copy in copies[:7]:
        copy.wait()
    seed, f_in, bias, f_out, decay, reach = local
    window = (table.shape[0] - block) // 2
    lags = window - block
    lag = lax.broadcasted_iota(jnp.int32, (lags, 1), 0)
    if seq_len & (seq_len - 1) == 0:
        phases = (lag * seed[...]) & (seq_len - 1)
    else:
        phases = lax.rem(lag * seed[...], seq_len)
    angles = phases.astype(jnp.float32).T * (2.0 * math.pi / seq_len)
    features = jnp.concatenate([jnp.cos(angles), jnp.sin(angles)], axis=0)
    dims = (((0,), (0,)), ((), ()))
    exact = dict(precision=lax.Precision.HIGHEST, preferred_element_type=jnp.float32)
    shift = jnp.broadcast_to(bias[...], (8, bias.shape[1])).T[:, :1]
    hidden = jnp.sin(lax.dot_general(f_in[...], features, dims, **exact) + shift)
    shaped = lax.dot_general(hidden, f_out[...], dims, **exact)
    envelope = jnp.exp(-decay[...] * lag.astype(jnp.float32)) * scale
    taps = jnp.where(lag < reach[...] * block, shaped * envelope, 0.0).astype(jnp.bfloat16).T
    spectrum[...] = jnp.dot(taps, table[:lags], preferred_element_type=jnp.float32) + jnp.dot(
        taps, table[window : window + lags], preferred_element_type=jnp.float32
    )
    for copy in copies[7:]:
        copy.wait()


def transform(places, xs, valid, table, start, tile):
    block = xs[0].shape[1]
    blocks = []
    for x, there in zip(xs, valid):
        rows = x[start : start + tile]
        blocks.append(rows if there is None else jnp.where(there, rows, jnp.zeros_like(rows)))
    factors = [table[place * block : (place + 1) * block] for place in places]
    return jnp.dot(
        jnp.concatenate(blocks, axis=1), jnp.concatenate(factors, axis=0), preferred_element_type=jnp.float32
    )


def block_there(window, block, place):
    back = window // block - 1 - place
    return None if back == 0 else lax.axis_index("seq") >= back


def respond(freq, group, per_group, window, spectrum, table):
    half = table.shape[1] // 2
    mult = []
    for g in range(freq.shape[0] // per_group):
        part = freq[g * per_group : (g + 1) * per_group]
        hc, hs = spectrum[group + g : group + g + 1, :half], spectrum[group + g : group + g + 1, half:]
        xc, xs = part[:, :half], part[:, half:]
        mult.append(jnp.concatenate([xc * hc - xs * hs, xc * hs + xs * hc], axis=1).astype(jnp.bfloat16))
    block = table.shape[0] - 2 * window
    both = lax.dot_general(
        jnp.concatenate(mult, axis=0),
        table[2 * window - block :],
        (((1,), (1,)), ((), ())),
        preferred_element_type=jnp.float32,
    )
    return both[:, :block] + both[:, block:]


def in_stages(channels, first, second):
    tiles = [(start, min(TILE, channels - start)) for start in range(0, channels, TILE)]
    ready = first(*tiles[0])
    for k, tile in enumerate(tiles):
        now = ready
        if k + 1 < len(tiles):
            ready = first(*tiles[k + 1])
        second(*tile, now)


def ahead_kernel(window, per_group, first, own, other, spectrum, table, out):
    even = lax.axis_index("seq") % 2 == 0

    def give(start, tile, freq):
        ahead = respond(freq, (first + start) // per_group, per_group, window, spectrum, table)
        out[start : start + tile] = ahead.astype(out.dtype)

    in_stages(out.shape[0], functools.partial(transform, (0, 1), (own, other), (None, even), table), give)


def gains(skip, row, block):
    gain = jnp.broadcast_to(skip[row : row + 1], (128, 128)).T
    return gain if block == 128 else jnp.broadcast_to(gain[:, :1], (128, block))


def base_kernel(window, places, odd_only, per_group, first, *refs):
    xs, (skip, spectrum, table, out) = refs[: len(places)], refs[len(places) :]
    block = out.shape[1]
    odd = lax.axis_index("seq") % 2 == 1
    valid = [odd if odd_only else block_there(window, block, place) for place in places[:-1]] + [None]

    def give(start, tile, freq):
        mixed = respond(freq, (first + start) // per_group, per_group, window, spectrum, table)
        for low in range(0, tile, 128):
            here = slice(start + low, start + low + 128)
            gain = gains(skip, (first + start + low) // 128, block)
            out[here] = mixed[low : low + 128] + gain * xs[-1][here].astype(jnp.float32)

    in_stages(out.shape[0], functools.partial(transform, places, xs, valid, table), give)


def column_halves(weight):
    cols = weight.shape[1] // 2
    core = lax.axis_index("chan")
    return [pl.ds(pl.multiple_of(part * cols, 128), cols) for part in (core, 1 - core)]


def gate(first, query, gated_t, start, mixed):
    rows = slice(start, start + mixed.shape[0])
    gated = query[first + start : first + start + mixed.shape[0]].astype(jnp.float32) * mixed
    gated_t[:, rows] = gated.astype(jnp.bfloat16).T


def first_block_kernel(splits, base_a, base_b, query, weight, gated_a, gated_b, part):
    there = column_halves(weight)[1]

    @pl.when(lax.axis_index("seq") == 0)
    def _():
        total = 0.0
        for first, base, gated_t in zip(splits, (base_a, base_b), (gated_a, gated_b)):
            channels = base.shape[0]
            for start in range(0, channels, 128):
                gate(first, query, gated_t, start, base[start : start + 128])
            total += jnp.dot(
                gated_t[...], weight[first : first + channels, there], preferred_element_type=jnp.float32
            )
        part[...] = total.astype(part.dtype)


def last_kernel(first, carried, base, query, weight, before, gated_in, part_in, gated_t, part):
    there = column_halves(weight)[1]
    seq = lax.axis_index("seq")

    @pl.when(seq > 0)
    def _():
        for start in range(0, base.shape[0], 128):
            rows = slice(start, start + 128)
            gate(first, query, gated_t, start, base[rows] + jnp.where(seq >= 2, carried[rows].astype(jnp.float32), 0.0))
        total = jnp.dot(gated_t[...], weight[first:, there], preferred_element_type=jnp.float32)
        part[...] = (before[...] + total).astype(part.dtype)


def hand_kernel(far, own, out):
    out[...] = jnp.where(lax.axis_index("seq") % 2 == 1, far[...], own[...])


def part_kernel(window, places, per_group, first, is_first, *refs):
    xs, refs = refs[: len(places)], refs[len(places) :]
    (base, query, spectrum, table, weight), refs = refs[:5], refs[5:]
    gated_t, part = refs[-2:]
    block, channels = gated_t.shape
    seq = lax.axis_index("seq")
    valid = [block_there(window, block, place) for place in places]
    there = column_halves(weight)[1]

    def add(start, tile, freq):
        mixed = respond(freq, (first + start) // per_group, per_group, window, spectrum, table)
        gate(first, query, gated_t, start, base[start : start + tile] + mixed)

    @pl.when(seq > 0)
    def _():
        in_stages(channels, functools.partial(transform, places, xs, valid, table), add)
        total = jnp.dot(gated_t[...], weight[first : first + channels, there], preferred_element_type=jnp.float32)
        if not is_first:
            total = refs[0][...] + total
        part[...] = total.astype(part.dtype)


def own_kernel(first, gated_t, weight, *refs):
    here = column_halves(weight)[0]
    rows = slice(first, first + gated_t.shape[1])
    total = jnp.dot(gated_t[...], weight[rows, here], preferred_element_type=jnp.float32)
    refs[-1][...] = total if len(refs) == 1 else refs[0][...] + total


def cost(bytes_accessed):
    return pl.CostEstimate(flops=1, bytes_accessed=bytes_accessed, transcendentals=0)


def shift(array, back, cyclic):
    count = lax.axis_size("seq")
    return lax.ppermute(array, "seq", [(i, (i + back) % count) for i in range(count if cyclic else count - back)])


def swap_pairs(array):
    return lax.ppermute(array, "seq", [(i, i ^ 1) for i in range(lax.axis_size("seq"))])


def body(
    query_feat,
    key_feat,
    value_feat,
    filter_seed,
    filter_in,
    filter_bias,
    filter_out,
    decay_rate,
    reach_blocks,
    skip_gain,
    out_weight,
):
    channels, block = query_feat.shape
    seq_count = lax.axis_size("seq")
    reach_max = seq_count // 4
    filters = decay_rate.shape[0]
    per_group = channels // filters
    lags = reach_max * block
    window = lags + block
    (fwd_hi, fwd_lo), (inv_hi, inv_lo) = transform_tables(window, lags, block)
    table = np.concatenate([fwd_hi, fwd_lo[:lags], inv_hi.T, inv_lo.T], axis=0)
    length = table.shape[1]
    out_cols = out_weight.shape[1]
    cols = out_cols // 2
    params = pltpu.CompilerParams(vmem_limit_bytes=VMEM_BYTES)
    vmem = pl.BlockSpec(memory_space=pltpu.VMEM)
    f32, bf16 = jnp.float32, jnp.bfloat16
    shape = jax.ShapeDtypeStruct

    products = [
        (key_feat[low:high].astype(f32) * value_feat[low:high].astype(f32)).astype(bf16)
        for low, high in ((0, RELAYED), (RELAYED, channels))
    ]
    if reach_max == 2:
        other = swap_pairs(products[1])
        far = shift(products[0], 2, WRAP_FAR)

    small = (
        filter_seed[None],
        filter_in,
        filter_bias[None],
        filter_out,
        decay_rate[None],
        reach_blocks[None],
    )
    large = (
        jnp.asarray(table),
        query_feat,
        skip_gain.reshape(-1, 128),
    )
    weight_in = pltpu.with_memory_space_constraint(out_weight, pltpu.HBM)
    spectrum, table, query, skip, weight = pl.pallas_call(
        lambda *refs: setup_kernel(block * seq_count, block, 1.0 / math.sqrt(lags), *refs),
        in_specs=[pl.BlockSpec(memory_space=pltpu.HBM)] * 10,
        out_specs=[vmem] * 5,
        out_shape=[pltpu.VMEM((filters, length), f32)] + [pltpu.VMEM(a.shape, a.dtype) for a in large]
        + [pltpu.VMEM(out_weight.shape, bf16)],
        scratch_shapes=[pltpu.VMEM(a.shape, a.dtype) for a in small] + [pltpu.SemaphoreType.DMA((10,))],
        compiler_params=params,
        cost_estimate=cost(SETUP_COST),
    )(*[pltpu.with_memory_space_constraint(a, pltpu.HBM) for a in small + large], weight_in)

    def kernel(call, ins, *outs, aliases={}):
        return pl.pallas_call(
            call,
            in_specs=[vmem] * len(ins),
            out_specs=[vmem] * len(outs),
            out_shape=outs,
            input_output_aliases=aliases,
            compiler_params=params,
            cost_estimate=cost(TAIL_COST),
        )(*ins)

    def base(first, blocks, odd_only=False):
        call = functools.partial(base_kernel, window, tuple(blocks), odd_only, per_group, first)
        return kernel(call, (*blocks.values(), skip, spectrum, table), shape(blocks[reach_max].shape, f32))[0]

    def first_block(base_a, base_b):
        shapes = [shape((block, base.shape[0]), bf16) for base in (base_a, base_b)]
        call = functools.partial(first_block_kernel, (0, RELAYED))
        return kernel(call, (base_a, base_b, query, weight), *shapes, shape((block, cols), bf16))

    def part(first, late, early, sums, gated, total=None):
        ins = (*late.values(), early, query, spectrum, table, weight, *sums, gated)
        aliases = {len(ins) - 1: 0}
        outs = [shape(gated.shape, bf16), shape((block, cols), f32)]
        if total is not None:
            aliases[len(ins)] = 1
            ins, outs[1] = (*ins, total), shape(total.shape, bf16)
        call = functools.partial(part_kernel, window, tuple(late), per_group, first, not sums)
        return kernel(call, ins, *outs, aliases=aliases)

    own_a, own_b = products
    if reach_max == 2:
        (sent,) = kernel(
            functools.partial(ahead_kernel, window, per_group, RELAYED),
            (own_b, other, spectrum, table),
            shape(own_b.shape, bf16),
        )
        carried = shift(sent, 2, WRAP_SENT)
        ready, _ = lax.optimization_barrier((own_a, spectrum))
        (handed,) = kernel(hand_kernel, (far, ready), shape(own_a.shape, bf16))
        near = swap_pairs(handed)
        base_a = base(0, {0: far, 2: own_a})
        base_b = base(RELAYED, {1: other, 2: own_b}, True)
        gated_a, gated_b, sums_b = first_block(base_a, base_b)
        gated_a, sums_a = part(0, {1: near}, base_a, (), gated_a)
        (own,) = kernel(functools.partial(own_kernel, 0), (gated_a, weight), shape((block, cols), f32))
        sums_a, own = lax.optimization_barrier((sums_a, own))
        gated_b, sums = kernel(
            functools.partial(last_kernel, RELAYED),
            (carried, base_b, query, weight, sums_a, gated_b, sums_b),
            shape(gated_b.shape, bf16),
            shape(sums_b.shape, bf16),
            aliases={5: 0, 6: 1},
        )
    else:
        halos = [{reach_max - back: shift(own, back, False) for back in range(1, reach_max + 1)} for own in products]
        base_a, base_b = base(0, {reach_max: own_a}), base(RELAYED, {reach_max: own_b})
        gated_a, gated_b, sums_b = first_block(base_a, base_b)
        gated_a, sums_a = part(0, halos[0], base_a, (), gated_a)
        (own,) = kernel(functools.partial(own_kernel, 0), (gated_a, weight), shape((block, cols), f32))
        gated_b, sums = part(RELAYED, halos[1], base_b, (sums_a,), gated_b, sums_b)
    received = lax.ppermute(sums, "chan", [(0, 1), (1, 0)])
    (own,) = kernel(functools.partial(own_kernel, RELAYED), (gated_b, weight, own), shape((block, cols), f32))
    return (own + received.astype(f32)).astype(bf16)


def solution(mesh):
    return jax.shard_map(
        body,
        mesh=mesh,
        in_specs=(
            P("chan", ("groups", "seq")),
            P("chan", ("groups", "seq")),
            P("chan", ("groups", "seq")),
            P(),
            P(),
            P(),
            P(None, "chan"),
            P("chan"),
            P("chan"),
            P("chan"),
            P("chan", None),
        ),
        out_specs=P(("groups", "seq"), "chan"),
        check_vma=False,
    )
```

```python
import functools
import math

import jax
import jax.numpy as jnp
import numpy as np
from jax import lax
from jax.experimental import pallas as pl
from jax.experimental.pallas import tpu as pltpu
from jax.sharding import PartitionSpec as P

SETUP_COST = 30_000_000
TAIL_COST = 1
VMEM_BYTES = 24 * 1024 * 1024
RELAYED = 1024
TILE = 512
WRAP_FAR = True
WRAP_SENT = False


def split_bf16(array):
    high = array.astype(jnp.bfloat16)
    low = (array - high.astype(np.float64)).astype(jnp.bfloat16)
    return high, low


def transform_tables(window, first_out, block):
    half = 128 * math.ceil(window / 256)
    omega = (np.arange(half) + 0.5) * (math.pi / half)
    angle = np.arange(window)[:, None] * omega[None, :]
    forward = np.concatenate([np.cos(angle), np.sin(angle)], axis=1)
    back = omega[:, None] * (first_out + np.arange(block))[None, :]
    inverse = np.concatenate([np.cos(back), np.sin(back)], axis=0) / half
    return split_bf16(forward), split_bf16(inverse)


def setup_kernel(seq_len, block, scale, *refs):
    small, weight, spectrum, weight_out, local, sems = refs[:6], refs[9], refs[10], refs[14], refs[15:21], refs[21]
    table = refs[11]
    pairs = list(zip(small, local)) + list(zip(refs[6:9], refs[11:14]))
    pairs.append((weight, weight_out))
    copies = [pltpu.make_async_copy(source, target, sems.at[k]) for k, (source, target) in enumerate(pairs)]
    for copy in copies:
        copy.start()
    for copy in copies[:7]:
        copy.wait()
    seed, f_in, bias, f_out, decay, reach = local
    window = table.shape[0] // 2
    lags = window - block
    lag = lax.broadcasted_iota(jnp.int32, (lags, 1), 0)
    if seq_len & (seq_len - 1) == 0:
        phases = (lag * seed[...]) & (seq_len - 1)
    else:
        phases = lax.rem(lag * seed[...], seq_len)
    angles = phases.astype(jnp.float32).T * (2.0 * math.pi / seq_len)
    features = jnp.concatenate([jnp.cos(angles), jnp.sin(angles)], axis=0)
    dims = (((0,), (0,)), ((), ()))
    exact = dict(precision=lax.Precision.HIGHEST, preferred_element_type=jnp.float32)
    shift = jnp.broadcast_to(bias[...], (8, bias.shape[1])).T[:, :1]
    hidden = jnp.sin(lax.dot_general(f_in[...], features, dims, **exact) + shift)
    shaped = lax.dot_general(hidden, f_out[...], dims, **exact)
    envelope = jnp.exp(-decay[...] * lag.astype(jnp.float32)) * scale
    taps = jnp.where(lag < reach[...] * block, shaped * envelope, 0.0).astype(jnp.bfloat16).T
    spectrum[...] = jnp.dot(taps, table[:lags], preferred_element_type=jnp.float32) + jnp.dot(
        taps, table[window : window + lags], preferred_element_type=jnp.float32
    )
    for copy in copies[7:]:
        copy.wait()


def transform(places, xs, valid, table, start, tile):
    block = xs[0].shape[1]
    blocks = []
    for x, there in zip(xs, valid):
        rows = x[start : start + tile]
        blocks.append(rows if there is None else jnp.where(there, rows, jnp.zeros_like(rows)))
    factors = [table[place * block : (place + 1) * block] for place in places]
    return jnp.dot(
        jnp.concatenate(blocks, axis=1), jnp.concatenate(factors, axis=0), preferred_element_type=jnp.float32
    )


def block_there(window, block, place):
    back = window // block - 1 - place
    return None if back == 0 else lax.axis_index("seq") >= back


def respond(freq, group, per_group, block, spectrum, table):
    half = table.shape[1] // 2
    mult = []
    for g in range(freq.shape[0] // per_group):
        part = freq[g * per_group : (g + 1) * per_group]
        hc, hs = spectrum[group + g : group + g + 1, :half], spectrum[group + g : group + g + 1, half:]
        xc, xs = part[:, :half], part[:, half:]
        mult.append(jnp.concatenate([xc * hc - xs * hs, xc * hs + xs * hc], axis=1).astype(jnp.bfloat16))
    return lax.dot_general(
        jnp.concatenate(mult, axis=0),
        table[table.shape[0] - block :],
        (((1,), (1,)), ((), ())),
        preferred_element_type=jnp.float32,
    )


def in_stages(channels, first, second):
    tiles = [(start, min(TILE, channels - start)) for start in range(0, channels, TILE)]
    ready = first(*tiles[0])
    for k, tile in enumerate(tiles):
        now = ready
        if k + 1 < len(tiles):
            ready = first(*tiles[k + 1])
        second(*tile, now)


def ahead_kernel(window, per_group, first, own, other, spectrum, table, out):
    even = lax.axis_index("seq") % 2 == 0

    def give(start, tile, freq):
        ahead = respond(freq, (first + start) // per_group, per_group, out.shape[1], spectrum, table)
        out[start : start + tile] = ahead.astype(out.dtype)

    in_stages(out.shape[0], functools.partial(transform, (0, 1), (own, other), (None, even), table), give)


def gains(skip, row, block):
    gain = jnp.broadcast_to(skip[row : row + 1], (128, 128)).T
    return gain if block == 128 else jnp.broadcast_to(gain[:, :1], (128, block))


def base_kernel(window, places, odd_only, per_group, first, *refs):
    xs, (skip, spectrum, table, out) = refs[: len(places)], refs[len(places) :]
    block = out.shape[1]
    odd = lax.axis_index("seq") % 2 == 1
    valid = [odd if odd_only else block_there(window, block, place) for place in places[:-1]] + [None]

    def give(start, tile, freq):
        mixed = respond(freq, (first + start) // per_group, per_group, block, spectrum, table)
        for low in range(0, tile, 128):
            here = slice(start + low, start + low + 128)
            gain = gains(skip, (first + start + low) // 128, block)
            out[here] = mixed[low : low + 128] + gain * xs[-1][here].astype(jnp.float32)

    in_stages(out.shape[0], functools.partial(transform, places, xs, valid, table), give)


def column_halves(weight):
    cols = weight.shape[1] // 2
    core = lax.axis_index("chan")
    return [pl.ds(pl.multiple_of(part * cols, 128), cols) for part in (core, 1 - core)]


def gate(first, query, gated_t, start, mixed):
    rows = slice(start, start + mixed.shape[0])
    gated = query[first + start : first + start + mixed.shape[0]].astype(jnp.float32) * mixed
    gated_t[:, rows] = gated.astype(jnp.bfloat16).T


def first_block_kernel(splits, base_a, base_b, query, weight, gated_a, gated_b, part):
    there = column_halves(weight)[1]

    @pl.when(lax.axis_index("seq") == 0)
    def _():
        total = 0.0
        for first, base, gated_t in zip(splits, (base_a, base_b), (gated_a, gated_b)):
            channels = base.shape[0]
            for start in range(0, channels, 128):
                gate(first, query, gated_t, start, base[start : start + 128])
            total += jnp.dot(
                gated_t[...], weight[first : first + channels, there], preferred_element_type=jnp.float32
            )
        part[...] = total.astype(part.dtype)


def last_kernel(first, carried, base, query, weight, before, gated_in, part_in, gated_t, part):
    there = column_halves(weight)[1]
    seq = lax.axis_index("seq")

    @pl.when(seq > 0)
    def _():
        for start in range(0, base.shape[0], 128):
            rows = slice(start, start + 128)
            gate(first, query, gated_t, start, base[rows] + jnp.where(seq >= 2, carried[rows].astype(jnp.float32), 0.0))
        total = jnp.dot(gated_t[...], weight[first:, there], preferred_element_type=jnp.float32)
        part[...] = (before[...] + total).astype(part.dtype)


def hand_kernel(far, own, out):
    out[...] = jnp.where(lax.axis_index("seq") % 2 == 1, far[...], own[...])


def part_kernel(window, places, per_group, first, is_first, *refs):
    xs, refs = refs[: len(places)], refs[len(places) :]
    (base, query, spectrum, table, weight), refs = refs[:5], refs[5:]
    gated_t, part = refs[-2:]
    block, channels = gated_t.shape
    seq = lax.axis_index("seq")
    valid = [block_there(window, block, place) for place in places]
    there = column_halves(weight)[1]

    def add(start, tile, freq):
        mixed = respond(freq, (first + start) // per_group, per_group, block, spectrum, table)
        gate(first, query, gated_t, start, base[start : start + tile] + mixed)

    @pl.when(seq > 0)
    def _():
        in_stages(channels, functools.partial(transform, places, xs, valid, table), add)
        total = jnp.dot(gated_t[...], weight[first : first + channels, there], preferred_element_type=jnp.float32)
        if not is_first:
            total = refs[0][...] + total
        part[...] = total.astype(part.dtype)


def own_kernel(gated_a, gated_b, weight, out):
    here = column_halves(weight)[0]
    gated_t = jnp.concatenate([gated_a[...], gated_b[...]], axis=1)
    out[...] = jnp.dot(gated_t, weight[:, here], preferred_element_type=jnp.float32)


def cost(bytes_accessed):
    return pl.CostEstimate(flops=1, bytes_accessed=bytes_accessed, transcendentals=0)


def shift(array, back, cyclic):
    count = lax.axis_size("seq")
    return lax.ppermute(array, "seq", [(i, (i + back) % count) for i in range(count if cyclic else count - back)])


def swap_pairs(array):
    return lax.ppermute(array, "seq", [(i, i ^ 1) for i in range(lax.axis_size("seq"))])


def body(
    query_feat,
    key_feat,
    value_feat,
    filter_seed,
    filter_in,
    filter_bias,
    filter_out,
    decay_rate,
    reach_blocks,
    skip_gain,
    out_weight,
):
    channels, block = query_feat.shape
    seq_count = lax.axis_size("seq")
    reach_max = seq_count // 4
    filters = decay_rate.shape[0]
    per_group = channels // filters
    lags = reach_max * block
    window = lags + block
    (fwd_hi, fwd_lo), (inv_hi, inv_lo) = transform_tables(window, lags, block)
    table = np.concatenate([fwd_hi, fwd_lo[:lags], inv_hi.T], axis=0)
    length = table.shape[1]
    out_cols = out_weight.shape[1]
    cols = out_cols // 2
    params = pltpu.CompilerParams(vmem_limit_bytes=VMEM_BYTES)
    vmem = pl.BlockSpec(memory_space=pltpu.VMEM)
    f32, bf16 = jnp.float32, jnp.bfloat16
    shape = jax.ShapeDtypeStruct

    products = [
        (key_feat[low:high].astype(f32) * value_feat[low:high].astype(f32)).astype(bf16)
        for low, high in ((0, RELAYED), (RELAYED, channels))
    ]
    if reach_max == 2:
        other = swap_pairs(products[1])
        far = shift(products[0], 2, WRAP_FAR)

    small = (
        filter_seed[None],
        filter_in,
        filter_bias[None],
        filter_out,
        decay_rate[None],
        reach_blocks[None],
    )
    large = (
        jnp.asarray(table),
        query_feat,
        skip_gain.reshape(-1, 128),
    )
    weight_in = pltpu.with_memory_space_constraint(out_weight, pltpu.HBM)
    spectrum, table, query, skip, weight = pl.pallas_call(
        lambda *refs: setup_kernel(block * seq_count, block, 1.0 / math.sqrt(lags), *refs),
        in_specs=[pl.BlockSpec(memory_space=pltpu.HBM)] * 10,
        out_specs=[vmem] * 5,
        out_shape=[pltpu.VMEM((filters, length), f32)] + [pltpu.VMEM(a.shape, a.dtype) for a in large]
        + [pltpu.VMEM(out_weight.shape, bf16)],
        scratch_shapes=[pltpu.VMEM(a.shape, a.dtype) for a in small] + [pltpu.SemaphoreType.DMA((10,))],
        compiler_params=params,
        cost_estimate=cost(SETUP_COST),
    )(*[pltpu.with_memory_space_constraint(a, pltpu.HBM) for a in small + large], weight_in)

    def kernel(call, ins, *outs, aliases={}):
        return pl.pallas_call(
            call,
            in_specs=[vmem] * len(ins),
            out_specs=[vmem] * len(outs),
            out_shape=outs,
            input_output_aliases=aliases,
            compiler_params=params,
            cost_estimate=cost(TAIL_COST),
        )(*ins)

    def base(first, blocks, odd_only=False):
        call = functools.partial(base_kernel, window, tuple(blocks), odd_only, per_group, first)
        return kernel(call, (*blocks.values(), skip, spectrum, table), shape(blocks[reach_max].shape, f32))[0]

    def first_block(base_a, base_b):
        shapes = [shape((block, base.shape[0]), bf16) for base in (base_a, base_b)]
        call = functools.partial(first_block_kernel, (0, RELAYED))
        return kernel(call, (base_a, base_b, query, weight), *shapes, shape((block, cols), bf16))

    def part(first, late, early, sums, gated, total=None):
        ins = (*late.values(), early, query, spectrum, table, weight, *sums, gated)
        aliases = {len(ins) - 1: 0}
        outs = [shape(gated.shape, bf16), shape((block, cols), f32)]
        if total is not None:
            aliases[len(ins)] = 1
            ins, outs[1] = (*ins, total), shape(total.shape, bf16)
        call = functools.partial(part_kernel, window, tuple(late), per_group, first, not sums)
        return kernel(call, ins, *outs, aliases=aliases)

    own_a, own_b = products
    if reach_max == 2:
        (sent,) = kernel(
            functools.partial(ahead_kernel, window, per_group, RELAYED),
            (own_b, other, spectrum, table),
            shape(own_b.shape, bf16),
        )
        carried = shift(sent, 2, WRAP_SENT)
        ready, _ = lax.optimization_barrier((own_a, spectrum))
        (handed,) = kernel(hand_kernel, (far, ready), shape(own_a.shape, bf16))
        near = swap_pairs(handed)
        base_a = base(0, {0: far, 2: own_a})
        base_b = base(RELAYED, {1: other, 2: own_b}, True)
        gated_a, gated_b, sums_b = first_block(base_a, base_b)
        gated_a, sums_a = part(0, {1: near}, base_a, (), gated_a)
        gated_b, sums = kernel(
            functools.partial(last_kernel, RELAYED),
            (carried, base_b, query, weight, sums_a, gated_b, sums_b),
            shape(gated_b.shape, bf16),
            shape(sums_b.shape, bf16),
            aliases={5: 0, 6: 1},
        )
    else:
        halos = [{reach_max - back: shift(own, back, False) for back in range(1, reach_max + 1)} for own in products]
        base_a, base_b = base(0, {reach_max: own_a}), base(RELAYED, {reach_max: own_b})
        gated_a, gated_b, sums_b = first_block(base_a, base_b)
        gated_a, sums_a = part(0, halos[0], base_a, (), gated_a)
        gated_b, sums = part(RELAYED, halos[1], base_b, (sums_a,), gated_b, sums_b)
    received = lax.ppermute(sums, "chan", [(0, 1), (1, 0)])
    (own,) = kernel(own_kernel, (gated_a, gated_b, weight), shape((block, cols), f32))
    return (own + received.astype(f32)).astype(bf16)


def solution(mesh):
    return jax.shard_map(
        body,
        mesh=mesh,
        in_specs=(
            P("chan", ("groups", "seq")),
            P("chan", ("groups", "seq")),
            P("chan", ("groups", "seq")),
            P(),
            P(),
            P(),
            P(None, "chan"),
            P("chan"),
            P("chan"),
            P("chan"),
            P("chan", None),
        ),
        out_specs=P(("groups", "seq"), "chan"),
        check_vma=False,
    )
```
